256 devices in a mesh: grp: 32 (over x, z), uly: 8 (over y, core).
Axes of the slice: x: 4, y: 4, z: 8, core: 2. Of those that a mesh axis runs over, the one named last changes fastest.
Arguments:
- tokens: bfloat16 [32768, 3072], P(('grp', 'uly')), may hold values from -60 to 60
- block_image: int32 [4096], P(('grp', 'uly')), may hold values from 0 to 63, as said below
- dest_slot: int32 [4096], P(('grp', 'uly')), may hold values from 0 to 15, as said below
- timestep: int32 [64], P('grp'), may hold values from 0 to 999
- txt_len: int32 [64], P('grp'), may hold values from 1 to 128
- mod_weight: bfloat16 [256, 9216], replicated, may hold values from -0.375 to 0.375
- qkv_weight: bfloat16 [3072, 6144], P('grp', 'uly'), may hold values from -0.109375 to 0.109375
- q_gain: float32 [128], replicated, may hold values from 1 to 2.5
- k_gain: float32 [128], replicated, may hold values from 1 to 2.5
- text_kv: bfloat16 [64, 128, 4096], P('grp', None, 'uly'), may hold values from -6 to 6
- out_weight: bfloat16 [2048, 3072], P(None, 'grp'), may hold values from -0.125 to 0.125
Outputs:
- update: bfloat16 [32768, 3072], P(('grp', 'uly'))
The draws below stay inside these ranges and needn't reach their ends.
Inputs may be any that keep to these rules, and one draw needn't show every extreme that they name: `block_image`: image i belongs to group i // 2, and every image has at least 256 tokens. The blocks of one device name images of any one group at most 1 times, and some device does so 1 times. `dest_slot`: A block keeps its uly index and goes to group block_image // 2; every block slot of every device receives exactly one block. Along a group's positions, uly index times 16 plus slot, each image's blocks are contiguous and images come in increasing order.
All inputs are finite; a program needn't handle non-finite values.
Results may differ from the reference program's by a relative error of at most 0.015.
Values may be sent and summed in bfloat16 or wider, within the bound.
No kernel may reach another device: no remote copies, remote signals or barrier semaphores. Data moves between devices by JAX's collectives and lax.ppermute only.
A program may use at most 128 MiB of HBM per device.

```python
import math
import jax
import jax.numpy as jnp
from jax import lax

D = 3072
HEADS = 16
HD = 128
TEMB = 256
TXT = 128
BLK = 8
MIN_TOK = 256
IMG_GRP = 2
BLK_DEV = 16
GTOK = 1024
IMAGES = 64
BLOCKS = 4096
TOKENS = 32768
N_GRP = 32
N_ULY = 8


def plan_tables(key):
    groups = N_GRP
    columns = N_ULY
    per_device = BLK_DEV
    per_group = per_device * columns
    least = MIN_TOK // BLK
    extra = per_group - IMG_GRP * least
    units = max(extra, 1)
    key_len, key_col = jax.random.split(jax.random.fold_in(key, 101))
    weights = jax.random.randint(jax.random.fold_in(key_len, 1), (groups, IMG_GRP), 1, 9)
    cumulative = jnp.cumsum(weights, axis=1)
    picks = jax.random.randint(jax.random.fold_in(key_len, 2), (groups, units), 0, cumulative[:, -1:])
    chosen = jnp.sum(picks[:, :, None] >= cumulative[:, None, :], axis=2)
    live = (jnp.arange(units) < extra).astype(jnp.int32)
    counts = jnp.sum((chosen[:, :, None] == jnp.arange(IMG_GRP)[None, None, :]).astype(jnp.int32) * live[None, :, None], axis=1)
    lengths = least + counts
    ends = jnp.cumsum(lengths, axis=1)
    positions = jnp.arange(per_group)
    image_at = jnp.sum(positions[None, :, None] >= ends[:, None, :], axis=2).astype(jnp.int32)

    def column(ckey):
        key_a, key_b, key_c, key_d = jax.random.split(ckey, 4)
        first = jax.random.permutation(key_a, groups)
        second = jax.random.permutation(key_b, groups)
        base = per_device // groups
        rest = per_device % groups
        table = base + ((first[:, None] + second[None, :]) % groups < rest).astype(jnp.int32)
        running = jnp.cumsum(table, axis=1)
        order = jnp.arange(per_device)
        ordered = jnp.sum(order[None, :, None] >= running[:, None, :], axis=2)
        shuffles = jax.vmap(lambda k: jax.random.permutation(k, per_device))(jax.random.split(key_c, groups))
        target = jnp.take_along_axis(ordered, shuffles, axis=1)
        flat = target.reshape(-1)
        hits = (flat[:, None] == jnp.arange(groups)[None, :]).astype(jnp.int32)
        rank = jnp.sum((jnp.cumsum(hits, axis=0) - hits) * hits, axis=1)
        spots = jax.vmap(lambda k: jax.random.permutation(k, per_device))(jax.random.split(key_d, groups))
        slot = spots[flat, rank].reshape(groups, per_device)
        return (target, slot)
    target, slot = jax.vmap(column)(jax.random.split(key_col, columns))
    target = target.transpose(1, 0, 2)
    slot = slot.transpose(1, 0, 2)
    spot = jnp.arange(columns)[None, :, None] * per_device + slot
    image = target * IMG_GRP + image_at[target, spot]
    return (image.reshape(-1).astype(jnp.int32), slot.reshape(-1).astype(jnp.int32))


def draw_block_image(key, part):
    shared = plan_tables(key)
    return shared[0]


def draw_dest_slot(key, part):
    shared = plan_tables(key)
    return shared[1]


def draw_txt_len(key, part):
    key = jax.random.fold_in(key, 5)
    key_a, key_b = jax.random.split(key)
    lens = jax.random.randint(key_a, (IMAGES,), 1, TXT + 1)
    where = jax.random.randint(key_b, (), 0, IMAGES)
    lens = lens.at[where].set(TXT)
    lens = lens.at[(where + 1) % IMAGES].set(1)
    return lens.astype(jnp.int32)


def draw_tokens(key, part):
    key = jax.random.fold_in(key, 3)
    key_a = jax.random.fold_in(key, 0)
    base = jax.random.normal(key_a, (TOKENS, D), jnp.float32)
    values = jnp.clip(base, -6.0, 6.0)
    return values.astype(jnp.bfloat16)


def plant(array, rng, low, top_value):
    extent = array.shape
    place = [jax.random.randint(jax.random.fold_in(rng, axis), (), 0, extent[axis]) for axis in range(len(extent))]
    array = array.at[tuple(place)].set(low)
    longest = extent.index(max(extent))
    place[longest] = (place[longest] + 1) % extent[longest]
    return array.at[tuple(place)].set(top_value)


def level_of(key, dims, cuts, low, high):
    level = 1.0
    for dim, shards_of in cuts:
        draws = jax.random.uniform(jax.random.fold_in(jax.random.fold_in(key, 6), dim), (shards_of,), jnp.float32, low / len(cuts), high / len(cuts))
        level = level * jnp.repeat(jnp.exp(draws), dims[dim] // shards_of).reshape((-1,) + (1,) * (len(dims) - 1 - dim))
    return level


def gaussian(own_key, extent, width, bound, cuts=(), kind=jnp.bfloat16):
    values = jax.random.normal(own_key, extent, jnp.float32) * width
    if len(cuts) > 0:
        values = level_of(own_key, extent, cuts, -0.22, 0.18) * values
    return jnp.clip(values, min=-bound, max=bound).astype(kind)


def setup_inputs(seed: int = 0) -> dict:
    splits = jax.random.split(jax.random.key(seed), 12)
    return {
        "tokens": draw_tokens(jax.random.fold_in(splits[11], 71), 0),
        "block_image": draw_block_image(jax.random.fold_in(splits[11], 71), 0),
        "dest_slot": draw_dest_slot(jax.random.fold_in(splits[11], 71), 0),
        "timestep": plant(jax.random.randint(splits[3], (IMAGES,), 0, 1000), jax.random.fold_in(splits[3], 1), 0, 999).astype(jnp.int32),
        "txt_len": draw_txt_len(jax.random.fold_in(splits[11], 71), 0),
        "mod_weight": gaussian(splits[5], (TEMB, 3 * D), TEMB ** -0.5, 0.375),
        "qkv_weight": gaussian(splits[6], (D, 3 * HEADS * HD), D ** -0.5, 0.109375, ((0, 32), (1, 8))),
        "q_gain": jnp.clip(jnp.exp(jax.random.uniform(splits[7], (HD,), jnp.float32, math.log(1.0), math.log(2.5))), 1.0, 2.5),
        "k_gain": jnp.clip(jnp.exp(jax.random.uniform(splits[8], (HD,), jnp.float32, math.log(1.0), math.log(2.5))), 1.0, 2.5),
        "text_kv": gaussian(splits[9], (IMAGES, TXT, 2 * HEADS * HD), 1.0, 6.0, ((0, 32), (2, 8))),
        "out_weight": gaussian(splits[10], (HEADS * HD, D), (HEADS * HD) ** -0.5, 0.125, ((1, 32),)),
    }


def layer_norm(values):
    mean = lax.optimization_barrier(jnp.mean(values, axis=-1, keepdims=True))
    centred = values - mean
    spread = lax.optimization_barrier(jnp.mean(centred * centred, axis=-1, keepdims=True))
    return centred * lax.rsqrt(spread + 1e-06)

def rms_scale(values, gain):
    return values * lax.rsqrt(lax.optimization_barrier(jnp.mean(values * values, axis=-1, keepdims=True)) + 1e-06) * gain

def modulation(timestep, mod_weight):
    half = mod_weight.shape[0] // 2
    freqs = jnp.exp(-math.log(10000.0) * jnp.arange(half, dtype=jnp.float32) / half)
    angles = timestep.astype(jnp.float32)[:, None] * freqs[None, :]
    embedded = jnp.concatenate([jnp.cos(angles), jnp.sin(angles)], axis=1)
    active = jax.nn.silu(embedded).astype(jnp.bfloat16)
    return jnp.dot(active, mod_weight, preferred_element_type=jnp.float32)

def select_rows(mods, owner):
    onehot = (owner[:, None] == jnp.arange(mods.shape[0], dtype=jnp.int32)[None, :]).astype(jnp.float32)
    return jnp.dot(onehot, mods, precision=lax.Precision.HIGHEST)

def head_attention(query, keys, values, q_owner, k_owner, k_live):
    scores = jnp.dot(query, keys.T, preferred_element_type=jnp.float32) * query.shape[-1] ** (-0.5)
    match = (q_owner[:, None] == k_owner[None, :]) & k_live[None, :]
    weights = jnp.where(match, jnp.exp(scores), 0.0)
    total = lax.optimization_barrier(jnp.sum(weights, axis=1, keepdims=True))
    summed = jnp.dot(weights.astype(jnp.bfloat16), values, preferred_element_type=jnp.float32)
    return (summed / total).astype(jnp.bfloat16)

def reference(tokens, block_image, dest_slot, timestep, txt_len, mod_weight, qkv_weight, q_gain, k_gain, text_kv, out_weight):
    images = block_image.reshape(N_GRP, N_ULY, BLK_DEV)
    slots = dest_slot.reshape(N_GRP, N_ULY, BLK_DEV)
    column = jnp.arange(N_ULY, dtype=jnp.int32)[None, :, None]
    target = (images // IMG_GRP * N_ULY + column) * BLK_DEV + slots
    target = target.reshape(-1).astype(jnp.int32)
    blocks = tokens.reshape(BLOCKS, BLK, D)
    moved = jnp.zeros_like(blocks).at[target].set(blocks).reshape(N_GRP, GTOK, D)
    owners = jnp.zeros((BLOCKS,), jnp.int32).at[target].set(images.reshape(-1) % IMG_GRP)
    owners = owners.reshape(N_GRP, BLK_DEV * N_ULY)

    def one_group(pack):
        rows, owner_blocks, steps_here, lens_here, text_here = pack
        mods = modulation(steps_here, mod_weight)
        owner = jnp.repeat(owner_blocks, BLK)
        picked = select_rows(mods, owner)
        shift = picked[:, :D]
        scale = picked[:, D:2 * D]
        gate = picked[:, 2 * D:]
        hidden = (layer_norm(rows.astype(jnp.float32)) * (1.0 + scale) + shift).astype(jnp.bfloat16)
        projected = jnp.dot(hidden, qkv_weight, preferred_element_type=jnp.float32).reshape(-1, HEADS, 3, HD)
        query = rms_scale(projected[:, :, 0], q_gain).astype(jnp.bfloat16)
        keys = rms_scale(projected[:, :, 1], k_gain).astype(jnp.bfloat16)
        values = projected[:, :, 2].astype(jnp.bfloat16)
        text = text_here.reshape(IMG_GRP, TXT, HEADS, 2, HD)
        text_key = rms_scale(text[:, :, :, 0].astype(jnp.float32), k_gain).astype(jnp.bfloat16)
        text_key = text_key.reshape(IMG_GRP * TXT, HEADS, HD)
        text_value = text[:, :, :, 1].reshape(IMG_GRP * TXT, HEADS, HD)
        all_keys = jnp.concatenate([keys, text_key], axis=0)
        all_values = jnp.concatenate([values, text_value], axis=0)
        text_owner = jnp.repeat(jnp.arange(IMG_GRP, dtype=jnp.int32), TXT)
        text_live = jnp.tile(jnp.arange(TXT, dtype=jnp.int32), IMG_GRP) < jnp.repeat(lens_here, TXT)
        k_owner = jnp.concatenate([owner, text_owner])
        k_live = jnp.concatenate([jnp.ones(owner.shape, bool), text_live])

        def per_head(trio):
            return head_attention(trio[0], trio[1], trio[2], owner, k_owner, k_live)
        mixed = lax.map(per_head, (query.transpose(1, 0, 2), all_keys.transpose(1, 0, 2), all_values.transpose(1, 0, 2)))
        mixed = mixed.transpose(1, 0, 2).reshape(-1, HEADS * HD)
        projection = jnp.dot(mixed, out_weight, preferred_element_type=jnp.float32)
        return (gate * projection).astype(jnp.bfloat16)
    result = lax.map(one_group, (moved, owners, timestep.reshape(N_GRP, IMG_GRP), txt_len.reshape(N_GRP, IMG_GRP), text_kv.reshape(N_GRP, IMG_GRP, TXT, 2 * HEADS * HD)))
    return result.reshape(TOKENS, D)
```

```python
import functools
import math

import jax
import jax.numpy as jnp
from jax import lax
from jax.experimental import pallas as pl
from jax.experimental.pallas import tpu as pltpu
from jax.sharding import PartitionSpec as P

HD = 128
TXT = 128
BLK = 8
IMG_GRP = 2
LANES = 128
BF16 = jnp.bfloat16
F32 = jnp.float32


def modulation(timestep, mod_weight):
    half = mod_weight.shape[0] // 2
    freqs = jnp.exp(-math.log(10000.0) * jnp.arange(half, dtype=F32) / half)
    angles = timestep.astype(F32)[:, None] * freqs[None, :]
    embedded = jnp.concatenate([jnp.cos(angles), jnp.sin(angles)], axis=1)
    active = jax.nn.silu(embedded).astype(BF16)
    return jnp.dot(active, mod_weight, preferred_element_type=F32)


def pack_kernel(image_ref, slot_ref, tokens_ref, out_ref):
    rows, width = tokens_ref.shape
    slots = out_ref.shape[0]
    lane_block = lax.broadcasted_iota(jnp.int32, (slots, rows), 1) // BLK
    row_block = lax.broadcasted_iota(jnp.int32, (rows, LANES), 0) // BLK
    target = jnp.zeros((slots, rows), jnp.int32)
    tags = jnp.zeros((rows, LANES), jnp.int32)
    for b in range(rows // BLK):
        image = image_ref[b]
        group = image // IMG_GRP
        tag = slot_ref[b] + 16 * (image - IMG_GRP * group) + 1
        target = jnp.where(lane_block == b, group * BLK, target)
        tags = jnp.where(row_block == b, tag, tags)
    target = target + lax.broadcasted_iota(jnp.int32, (slots, rows), 1) % BLK
    place = (lax.broadcasted_iota(jnp.int32, (slots, rows), 0) == target).astype(F32).astype(BF16)
    for start in range(0, width, 512):
        cols = slice(start, start + 512)
        out_ref[:, cols] = jnp.dot(place, tokens_ref[:, cols], preferred_element_type=F32).astype(BF16)
    out_ref[:, width:] = jnp.dot(place, tags.astype(F32).astype(BF16), preferred_element_type=F32).astype(BF16)


def norm_kernel(arrived_ref, mods_ref, out_ref, x_ref):
    slots = arrived_ref.shape[0]
    rows, width = x_ref.shape
    tags = arrived_ref[:, width:].astype(F32)
    lane_tag = tags.T.astype(jnp.int32)
    lane = lax.broadcasted_iota(jnp.int32, (rows, slots), 1)
    target = ((lane_tag - 1) % 16) * BLK + lane % BLK
    hit = (lax.broadcasted_iota(jnp.int32, (rows, slots), 0) == target) & (lane_tag > 0)
    place = hit.astype(F32).astype(BF16)
    for start in range(0, width, 512):
        cols = slice(start, start + 512)
        x_ref[:, cols] = jnp.dot(place, arrived_ref[:, cols], preferred_element_type=F32)
    placed_tag = jnp.dot(place, arrived_ref[:, width:], preferred_element_type=F32)
    owner = (placed_tag > 16.5).astype(F32)
    second = owner[:, :1] > 0.5
    values = x_ref[...]
    mean = jnp.mean(values, axis=-1, keepdims=True)
    centred = values - mean
    spread = jnp.mean(centred * centred, axis=-1, keepdims=True)
    scale_by = lax.rsqrt(spread + 1e-06)
    for start in range(0, width, 512):
        cols = slice(start, start + 512)
        s_cols = slice(width + start, width + start + 512)
        shift = jnp.where(second, mods_ref[1:2, cols], mods_ref[0:1, cols])
        scale = jnp.where(second, mods_ref[1:2, s_cols], mods_ref[0:1, s_cols])
        normed = (x_ref[:, cols] - mean) * scale_by
        out_ref[:, cols] = (normed * (1.0 + scale) + shift).astype(BF16)
    out_ref[:, width:] = owner.astype(BF16)


def rms(values, gain):
    return values * lax.rsqrt(jnp.mean(values * values, axis=-1, keepdims=True) + 1e-06) * gain


def attention_kernel(pieces, tile, u_ref, len_ref, *refs):
    hidden_refs = refs[: len(pieces)]
    w_hbm, qg_ref, kg_ref, text_ref, out_ref = refs[len(pieces) : len(pieces) + 5]
    x_ref, w_ref, q_ref, k_ref, v_ref, w_sem, x_sem = refs[len(pieces) + 5 :]
    tokens, full = x_ref.shape
    width = w_ref.shape[0]
    heads = w_ref.shape[1] // (3 * HD)
    keys = k_ref.shape[1]
    w_copy = pltpu.make_async_copy(w_hbm.at[:, pl.ds(0, 3 * heads * HD)], w_ref, w_sem)
    w_copy.start()
    copies = []
    for i, (ref, (start, size)) in enumerate(zip(hidden_refs, pieces)):
        copies.append(pltpu.make_async_copy(ref, x_ref.at[pl.ds(start, size)], x_sem.at[i]))
        copies[-1].start()
    q_gain = qg_ref[...]
    k_gain = kg_ref[...]
    for h in range(heads):
        for i in range(IMG_GRP):
            at = tokens + i * TXT
            key = text_ref[i, :, 2 * h * HD : (2 * h + 1) * HD].astype(F32)
            k_ref[h, at : at + TXT, :] = rms(key, k_gain).astype(BF16)
            v_ref[h, at : at + TXT, :] = text_ref[i, :, (2 * h + 1) * HD : (2 * h + 2) * HD]
    w_copy.wait()
    for copy in copies:
        copy.wait()
    for start in range(0, tokens, 512):
        rows = slice(start, start + 512)
        proj = jnp.dot(x_ref[rows, :width], w_ref[...], preferred_element_type=F32)
        for h in range(heads):
            at = 3 * h * HD
            q_ref[h, rows, :] = rms(proj[:, at : at + HD], q_gain).astype(BF16)
            k_ref[h, rows, :] = rms(proj[:, at + HD : at + 2 * HD], k_gain).astype(BF16)
            v_ref[h, rows, :] = proj[:, at + 2 * HD : at + 3 * HD].astype(BF16)
    lane = lax.broadcasted_iota(jnp.int32, (1, TXT), 1)
    codes = []
    for start in range(0, tokens, LANES):
        codes.append(x_ref[start : start + LANES, width:].astype(F32).T[:1])
    for i in range(IMG_GRP):
        codes.append(jnp.where(lane < len_ref[i], float(i), 2.0))
    code = jnp.concatenate(codes, axis=1)
    u = u_ref[0]
    for start in range(0, tokens, tile):
        rows = slice(start, start + tile)
        match = x_ref[rows, width : width + 1].astype(F32) == code
        for h in range(heads):
            scores = lax.dot_general(
                q_ref[h, rows, :], k_ref[h], (((1,), (1,)), ((), ())), preferred_element_type=F32
            ) * (HD ** -0.5)
            weights = jnp.where(match, jnp.exp(scores), 0.0)
            total = jnp.sum(weights, axis=1, keepdims=True)
            summed = jnp.dot(weights.astype(BF16), v_ref[h], preferred_element_type=F32)
            mixed = (summed / total).astype(BF16)
            for part in range(tile // 128):
                number = start // 128 + part
                offset = (0, 6, 2, 4)[number // 2]
                there = (u + offset) % 8
                if number % 2:
                    there = there + 1 - 2 * (there % 2)
                out_ref[there, :, h * HD : (h + 1) * HD] = mixed[part * 128 : part * 128 + 128]


def out_kernel(core_ref, mixed_ref, own_ref, other_ref, gate_ref, owner_ref, out_ref):
    half = own_ref.shape[1] // 256
    core = core_ref[0]
    total = jnp.zeros(out_ref.shape, F32)
    for i in range(half):
        cols = slice(i * 256, i * 256 + 256)
        for ref, side in ((own_ref, core), (other_ref, 1 - core)):
            total += lax.dot_general(
                mixed_ref[side * half + i], ref[:, cols], (((1,), (1,)), ((), ())), preferred_element_type=F32
            )
    second = owner_ref[:, :1].astype(F32) > 0.5
    gate = jnp.where(second, gate_ref[1:2, :], gate_ref[0:1, :])
    out_ref[...] = (gate * total).astype(BF16)


VMEM = pl.BlockSpec(memory_space=pltpu.VMEM)
SMEM = pl.BlockSpec(memory_space=pltpu.SMEM)
ANY = pl.BlockSpec(memory_space=pl.ANY)


def body(tokens, block_image, dest_slot, timestep, txt_len, mod_weight, qkv_weight, q_gain, k_gain, text_kv, out_weight):
    groups = lax.axis_size("grp")
    members = lax.axis_size("uly")
    u = lax.axis_index("uly").astype(jnp.int32)
    core = u % 2
    rows, width = tokens.shape
    heads = qkv_weight.shape[1] // (3 * HD)
    depth = out_weight.shape[0]
    group_tokens = rows * members

    out_t = lax.dynamic_slice_in_dim(out_weight.T, core * (depth // 2), depth // 2, axis=1)
    gathered = lax.all_gather(jnp.concatenate([qkv_weight, out_t], axis=1), "grp", axis=0, tiled=True)

    outgoing = pl.pallas_call(
        pack_kernel,
        out_shape=jax.ShapeDtypeStruct((groups * BLK, width + LANES), BF16),
        in_specs=[SMEM, SMEM, VMEM],
        out_specs=VMEM,
        compiler_params=pltpu.CompilerParams(vmem_limit_bytes=24 << 20),
        name="pack",
    )(block_image, dest_slot, tokens)
    arrived = lax.all_to_all(outgoing, "grp", split_axis=0, concat_axis=0, tiled=True)
    mods = modulation(timestep, mod_weight)
    hidden = pl.pallas_call(
        norm_kernel,
        out_shape=jax.ShapeDtypeStruct((rows, width + LANES), BF16),
        in_specs=[VMEM, VMEM],
        out_specs=VMEM,
        scratch_shapes=[pltpu.VMEM((rows, width), F32)],
        compiler_params=pltpu.CompilerParams(vmem_limit_bytes=24 << 20),
        name="norm",
    )(arrived, mods[:, : 2 * width])

    up = [(i, (i + 2) % members) for i in range(members)]
    down = [(i, (i - 2) % members) for i in range(members)]
    swap = [(i, i ^ 1) for i in range(members)]
    below = lax.ppermute(hidden, "uly", up)
    above = lax.ppermute(hidden, "uly", down)
    far_a = lax.ppermute(below[: rows // 2], "uly", up)
    far_b = lax.ppermute(above[rows // 2 :], "uly", down)
    parts, pieces = [], []
    at = 0
    for mine in ((hidden,), (below,), (above,), (far_a, far_b)):
        for side in (mine, tuple(lax.ppermute(m, "uly", swap) for m in mine)):
            for m in side:
                parts.append(m)
                pieces.append((at, m.shape[0]))
                at += m.shape[0]

    mixed = pl.pallas_call(
        functools.partial(attention_kernel, tuple(pieces), 256),
        out_shape=jax.ShapeDtypeStruct((members, rows, heads * HD), BF16),
        in_specs=[SMEM, SMEM] + [ANY] * (len(parts) + 1) + [VMEM, VMEM, VMEM],
        out_specs=VMEM,
        scratch_shapes=[
            pltpu.VMEM((group_tokens, width + LANES), BF16),
            pltpu.VMEM((width, 3 * heads * HD), BF16),
            pltpu.VMEM((heads, group_tokens, HD), BF16),
            pltpu.VMEM((heads, group_tokens + IMG_GRP * TXT, HD), BF16),
            pltpu.VMEM((heads, group_tokens + IMG_GRP * TXT, HD), BF16),
            pltpu.SemaphoreType.DMA,
            pltpu.SemaphoreType.DMA((len(parts),)),
        ],
        compiler_params=pltpu.CompilerParams(vmem_limit_bytes=48 << 20),
        name="attention",
    )(u.reshape(1), txt_len, *parts, gathered, q_gain.reshape(1, HD), k_gain.reshape(1, HD), text_kv)

    own_half = gathered[:, 3 * heads * HD :]
    other_half = lax.ppermute(own_half, "uly", swap)
    exchanged = lax.all_to_all(mixed, "uly", split_axis=0, concat_axis=0, tiled=True)
    block = 512
    return pl.pallas_call(
        out_kernel,
        grid=(width // block,),
        out_shape=jax.ShapeDtypeStruct((rows, width), BF16),
        in_specs=[
            SMEM,
            pl.BlockSpec(exchanged.shape, lambda n: (0, 0, 0)),
            pl.BlockSpec((block, depth // 2), lambda n: (n, 0)),
            pl.BlockSpec((block, depth // 2), lambda n: (n, 0)),
            pl.BlockSpec((IMG_GRP, block), lambda n: (0, 2 * width // block + n)),
            pl.BlockSpec((rows, LANES), lambda n: (0, width // LANES)),
        ],
        out_specs=pl.BlockSpec((rows, block), lambda n: (0, n)),
        compiler_params=pltpu.CompilerParams(vmem_limit_bytes=32 << 20),
        name="out",
    )(core.reshape(1), exchanged, own_half, other_half, mods, hidden)


def solution(mesh):
    return jax.shard_map(
        body,
        mesh=mesh,
        in_specs=(
            P(("grp", "uly"), None),
            P(("grp", "uly")),
            P(("grp", "uly")),
            P("grp"),
            P("grp"),
            P(),
            P("grp", "uly"),
            P(),
            P(),
            P("grp", None, "uly"),
            P(None, "grp"),
        ),
        out_specs=P(("grp", "uly"), None),
        check_vma=False,
    )
```

```python
import functools
import math

import jax
import jax.numpy as jnp
from jax import lax
from jax.experimental import pallas as pl
from jax.experimental.pallas import tpu as pltpu
from jax.sharding import PartitionSpec as P

HD = 128
TXT = 128
BLK = 8
IMG_GRP = 2
LANES = 128
BF16 = jnp.bfloat16
F32 = jnp.float32


def modulation(timestep, mod_weight):
    half = mod_weight.shape[0] // 2
    freqs = jnp.exp(-math.log(10000.0) * jnp.arange(half, dtype=F32) / half)
    angles = timestep.astype(F32)[:, None] * freqs[None, :]
    embedded = jnp.concatenate([jnp.cos(angles), jnp.sin(angles)], axis=1)
    active = jax.nn.silu(embedded).astype(BF16)
    return jnp.dot(active, mod_weight, preferred_element_type=F32)


def pack_kernel(image_ref, slot_ref, core_ref, tokens_hbm, out_w_hbm, out_hbm, half_hbm, *refs):
    tok_ref, buf_ref, half_ref, in_sem, out_sem, w_sem = refs
    rows, width = tok_ref.shape
    slots = buf_ref.shape[0]
    chunk = width // 3
    loads, weights = [], []
    for i in range(4):
        source = out_w_hbm.at[:, pl.ds(pl.multiple_of((2 * i + core_ref[0]) * 256, 256), 256)]
        weights.append(pltpu.make_async_copy(source, half_ref.at[:, pl.ds(i * 256, 256)], w_sem.at[i]))
    for i in range(3):
        part = pl.ds(i * chunk, chunk)
        loads.append(pltpu.make_async_copy(tokens_hbm.at[:, part], tok_ref.at[:, part], in_sem.at[i]))
    for copy in weights + loads:
        copy.start()
    for copy in weights:
        copy.wait()
    half_copy = pltpu.make_async_copy(half_ref, half_hbm, w_sem.at[4])
    half_copy.start()
    lane_block = lax.broadcasted_iota(jnp.int32, (slots, rows), 1) // BLK
    row_block = lax.broadcasted_iota(jnp.int32, (rows, LANES), 0) // BLK
    target = jnp.zeros((slots, rows), jnp.int32)
    tags = jnp.zeros((rows, LANES), jnp.int32)
    for b in range(rows // BLK):
        image = image_ref[b]
        group = image // IMG_GRP
        tag = slot_ref[b] + 16 * (image - IMG_GRP * group) + 1
        target = jnp.where(lane_block == b, group * BLK, target)
        tags = jnp.where(row_block == b, tag, tags)
    target = target + lax.broadcasted_iota(jnp.int32, (slots, rows), 1) % BLK
    place = (lax.broadcasted_iota(jnp.int32, (slots, rows), 0) == target).astype(F32).astype(BF16)
    stores = []
    for i in range(3):
        cols = slice(i * chunk, i * chunk + chunk)
        stop = i * chunk + chunk
        if i == 2:
            buf_ref[:, width:] = jnp.dot(place, tags.astype(F32).astype(BF16), preferred_element_type=F32).astype(BF16)
            stop = width + LANES
        loads[i].wait()
        buf_ref[:, cols] = jnp.dot(place, tok_ref[:, cols], preferred_element_type=F32).astype(BF16)
        part = pl.ds(i * chunk, stop - i * chunk)
        stores.append(pltpu.make_async_copy(buf_ref.at[:, part], out_hbm.at[:, part], out_sem.at[i]))
        stores[-1].start()
    for copy in stores + [half_copy]:
        copy.wait()


def norm_kernel(arrived_ref, mods_ref, out_ref, x_ref):
    slots = arrived_ref.shape[0]
    rows, width = x_ref.shape
    tags = arrived_ref[:, width:].astype(F32)
    lane_tag = tags.T.astype(jnp.int32)
    lane = lax.broadcasted_iota(jnp.int32, (rows, slots), 1)
    target = ((lane_tag - 1) % 16) * BLK + lane % BLK
    hit = (lax.broadcasted_iota(jnp.int32, (rows, slots), 0) == target) & (lane_tag > 0)
    place = hit.astype(F32).astype(BF16)
    for start in range(0, width, 512):
        cols = slice(start, start + 512)
        x_ref[:, cols] = jnp.dot(place, arrived_ref[:, cols], preferred_element_type=F32)
    placed_tag = jnp.dot(place, arrived_ref[:, width:], preferred_element_type=F32)
    owner = (placed_tag > 16.5).astype(F32)
    second = owner[:, :1] > 0.5
    values = x_ref[...]
    mean = jnp.mean(values, axis=-1, keepdims=True)
    centred = values - mean
    spread = jnp.mean(centred * centred, axis=-1, keepdims=True)
    scale_by = lax.rsqrt(spread + 1e-06)
    for start in range(0, width, 512):
        cols = slice(start, start + 512)
        s_cols = slice(width + start, width + start + 512)
        shift = jnp.where(second, mods_ref[1:2, cols], mods_ref[0:1, cols])
        scale = jnp.where(second, mods_ref[1:2, s_cols], mods_ref[0:1, s_cols])
        normed = (x_ref[:, cols] - mean) * scale_by
        out_ref[:, cols] = (normed * (1.0 + scale) + shift).astype(BF16)
    out_ref[:, width:] = owner.astype(BF16)


def rms(values, gain):
    return values * lax.rsqrt(jnp.mean(values * values, axis=-1, keepdims=True) + 1e-06) * gain


def attention_kernel(pieces, w_pieces, tile, x_axis_ref, len_ref, *refs):
    hidden_refs, refs = refs[: len(pieces)], refs[len(pieces) :]
    w_refs, refs = refs[: len(w_pieces)], refs[len(w_pieces) :]
    qg_ref, kg_ref, text_ref = refs[:3]
    out_refs = refs[3:7]
    x_ref, w_ref, q_ref, k_ref, v_ref, x_sem, w_sem = refs[7:]
    tokens, full = x_ref.shape
    width = w_ref.shape[0]
    heads = w_ref.shape[1] // (3 * HD)
    w_copies = []
    for i, (ref, (dx, start)) in enumerate(zip(w_refs, w_pieces)):
        row = pl.multiple_of((x_axis_ref[0] + dx) % 4 * (width // 4) + start, 16)
        w_copies.append(pltpu.make_async_copy(ref, w_ref.at[pl.ds(row, ref.shape[0])], w_sem.at[i]))
        w_copies[-1].start()
    copies = []
    for i, (ref, (start, size)) in enumerate(zip(hidden_refs, pieces)):
        copies.append(pltpu.make_async_copy(ref, x_ref.at[pl.ds(start, size)], x_sem.at[i]))
        copies[-1].start()
    q_gain = qg_ref[...]
    k_gain = kg_ref[...]
    for h in range(heads):
        for i in range(IMG_GRP):
            at = tokens + i * TXT
            key = text_ref[i, :, 2 * h * HD : (2 * h + 1) * HD].astype(F32)
            k_ref[h, at : at + TXT, :] = rms(key, k_gain).astype(BF16)
            v_ref[h, at : at + TXT, :] = text_ref[i, :, (2 * h + 1) * HD : (2 * h + 2) * HD]
    for copy in w_copies:
        copy.wait()
    for start in range(0, tokens, 512):
        rows = slice(start, start + 512)
        for copy, (at, size) in zip(copies, pieces):
            if start <= at < start + 512:
                copy.wait()
        proj = jnp.dot(x_ref[rows, :width], w_ref[...], preferred_element_type=F32)
        for h in range(heads):
            at = 3 * h * HD
            q_ref[h, rows, :] = rms(proj[:, at : at + HD], q_gain).astype(BF16)
            k_ref[h, rows, :] = rms(proj[:, at + HD : at + 2 * HD], k_gain).astype(BF16)
            v_ref[h, rows, :] = proj[:, at + 2 * HD : at + 3 * HD].astype(BF16)
    lane = lax.broadcasted_iota(jnp.int32, (1, TXT), 1)
    codes = []
    for start in range(0, tokens, LANES):
        codes.append(x_ref[start : start + LANES, width:].astype(F32).T[:1])
    for i in range(IMG_GRP):
        codes.append(jnp.where(lane < len_ref[i], float(i), 2.0))
    code = jnp.concatenate(codes, axis=1)
    for start in range(0, tokens, tile):
        rows = slice(start, start + tile)
        match = x_ref[rows, width : width + 1].astype(F32) == code
        for h in range(heads):
            scores = lax.dot_general(
                q_ref[h, rows, :], k_ref[h], (((1,), (1,)), ((), ())), preferred_element_type=F32
            )
            weights = jnp.where(match, jnp.exp2(scores * (HD ** -0.5 * math.log2(math.e))), 0.0)
            total = jnp.sum(weights, axis=1, keepdims=True)
            summed = jnp.dot(weights.astype(BF16), v_ref[h], preferred_element_type=F32)
            out_refs[start // tile][:, h * HD : (h + 1) * HD] = (summed / total).astype(BF16)


def out_kernel(offsets, me_ref, own_ref, *refs):
    others, (w_hbm, keep_ref, send_ref, m_ref, w_ref, sem) = refs[:3], refs[3:]
    half = keep_ref.shape[0]
    part = w_ref.shape[0] // 4
    block = part // 8
    copies = []
    for i, dx in enumerate(offsets):
        copies.append([])
        for z in range(8):
            row = pl.multiple_of(((me_ref[0] + dx) % 4 * 8 + z) * block, 16)
            source = w_hbm.at[pl.ds((z * len(offsets) + i) * block, block)]
            copies[i].append(pltpu.make_async_copy(source, w_ref.at[pl.ds(row, block)], sem.at[i * 8 + z]))
            copies[i][z].start()
    for ref, offset in zip((own_ref,) + others, (0, 1, 3, 2)):
        at = pl.multiple_of((me_ref[1] + offset) % 4 * 256, 256)
        m_ref[:, pl.ds(at, 256)] = ref[...]
    for i, dx in enumerate(offsets):
        for copy in copies[i]:
            copy.wait()
        cols = pl.ds(pl.multiple_of((me_ref[0] + dx) % 4 * part, part), part)
        total = lax.dot_general(m_ref[...], w_ref[cols, :], (((1,), (1,)), ((), ())), preferred_element_type=F32)
        keep_ref[:, cols] = total[:half]
        send_ref[:, cols] = total[half:].astype(BF16)


def gate_kernel(keep_ref, came_ref, owner_ref, gate_ref, out_ref):
    second = owner_ref[:, :1].astype(F32) > 0.5
    gate = jnp.where(second, gate_ref[1:2, :], gate_ref[0:1, :])
    out_ref[...] = (gate * (keep_ref[...] + came_ref[...].astype(F32))).astype(BF16)


VMEM = pl.BlockSpec(memory_space=pltpu.VMEM)
SMEM = pl.BlockSpec(memory_space=pltpu.SMEM)
HBM = pl.BlockSpec(memory_space=pltpu.HBM)


def body(tokens, block_image, dest_slot, timestep, txt_len, mod_weight, qkv_weight, q_gain, k_gain, text_kv, out_weight):
    groups = lax.axis_size("grp")
    members = lax.axis_size("uly")
    u = lax.axis_index("uly").astype(jnp.int32)
    core = u % 2
    g = lax.axis_index("grp").astype(jnp.int32)
    rows, width = tokens.shape
    heads = qkv_weight.shape[1] // (3 * HD)
    depth = out_weight.shape[0]
    group_tokens = rows * members

    w_rows, wide = qkv_weight.shape
    outgoing, out_half = pl.pallas_call(
        pack_kernel,
        out_shape=[
            jax.ShapeDtypeStruct((groups * BLK, width + LANES), BF16),
            jax.ShapeDtypeStruct((w_rows, depth // 2), BF16),
        ],
        in_specs=[SMEM, SMEM, SMEM, HBM, HBM],
        out_specs=[HBM, HBM],
        scratch_shapes=[
            pltpu.VMEM((rows, width), BF16),
            pltpu.VMEM((groups * BLK, width + LANES), BF16),
            pltpu.VMEM((w_rows, depth // 2), BF16),
            pltpu.SemaphoreType.DMA((3,)),
            pltpu.SemaphoreType.DMA((3,)),
            pltpu.SemaphoreType.DMA((5,)),
        ],
        compiler_params=pltpu.CompilerParams(vmem_limit_bytes=60 << 20),
        name="pack",
    )(block_image, dest_slot, core.reshape(1), tokens, out_weight.T)

    def shift(dx, dz):
        return [(x * 8 + z, (x + dx) % 4 * 8 + (z + dz) % 8) for x in range(4) for z in range(8)]

    z_groups = [[x * 8 + z for z in range(8)] for x in range(4)]
    z_line = lax.all_gather(qkv_weight, "grp", axis=0, tiled=True, axis_index_groups=z_groups)
    arrived = lax.all_to_all(outgoing, "grp", split_axis=0, concat_axis=0, tiled=True)
    offsets = (0, -1, -2, -3)
    x_line = jnp.concatenate(
        [out_half] + [lax.ppermute(out_half, "grp", shift(-dx, 0)) for dx in offsets[1:]], axis=0
    )
    out_rows = lax.all_gather(x_line, "grp", axis=0, tiled=True, axis_index_groups=z_groups)
    mods = modulation(timestep, mod_weight)
    hidden = pl.pallas_call(
        norm_kernel,
        out_shape=jax.ShapeDtypeStruct((rows, width + LANES), BF16),
        in_specs=[VMEM, VMEM],
        out_specs=VMEM,
        scratch_shapes=[pltpu.VMEM((rows, width), F32)],
        compiler_params=pltpu.CompilerParams(vmem_limit_bytes=24 << 20),
        cost_estimate=pl.CostEstimate(flops=69_000_000_000, bytes_accessed=2_000_000, transcendentals=0),
        name="norm",
    )(arrived, mods[:, : 2 * width])

    up = [(i, (i + 2) % members) for i in range(members)]
    down = [(i, (i - 2) % members) for i in range(members)]
    swap = [(i, i ^ 1) for i in range(members)]
    half_rows = rows // 2
    tie = lax.optimization_barrier
    x_below = lax.ppermute(z_line, "grp", shift(1, 0))
    x_above = lax.ppermute(z_line, "grp", shift(-1, 0))
    below = lax.ppermute(hidden, "uly", up)
    above = lax.ppermute(hidden, "uly", down)
    beside = lax.ppermute(hidden, "uly", swap)
    below, above, beside, x_below, x_above = tie((below, above, beside, x_below, x_above))
    far_a = lax.ppermute(below[:half_rows], "uly", up)
    far_b = lax.ppermute(above[half_rows:], "uly", down)
    below_s = lax.ppermute(below, "uly", swap)
    half_line = z_line.shape[0] // 2
    x_far_a = lax.ppermute(x_below[:half_line], "grp", shift(1, 0))
    x_far_b = lax.ppermute(x_above[half_line:], "grp", shift(-1, 0))
    far_a, far_b, below_s, above, x_far_a, x_far_b = tie((far_a, far_b, below_s, above, x_far_a, x_far_b))
    above_s = lax.ppermute(above, "uly", swap)
    far_as = lax.ppermute(far_a, "uly", swap)
    far_bs = lax.ppermute(far_b, "uly", swap)
    w_parts = [z_line, x_below, x_above, x_far_a, x_far_b]
    w_pieces = ((0, 0), (3, 0), (1, 0), (2, 0), (2, half_line))
    parts = [hidden, beside, below, below_s, above, above_s, far_a, far_b, far_as, far_bs]
    pieces, at = [], 0
    for part in parts:
        pieces.append((at, part.shape[0]))
        at += part.shape[0]
    chip = 2 * rows
    mixed = pl.pallas_call(
        functools.partial(attention_kernel, tuple(pieces), w_pieces, chip),
        out_shape=[jax.ShapeDtypeStruct((chip, heads * HD), BF16)] * 4,
        in_specs=[SMEM, SMEM] + [HBM] * (len(parts) + len(w_parts)) + [VMEM, VMEM, VMEM],
        out_specs=[VMEM] * 4,
        scratch_shapes=[
            pltpu.VMEM((group_tokens, width + LANES), BF16),
            pltpu.VMEM((width, 3 * heads * HD), BF16),
            pltpu.VMEM((heads, group_tokens, HD), BF16),
            pltpu.VMEM((heads, group_tokens + IMG_GRP * TXT, HD), BF16),
            pltpu.VMEM((heads, group_tokens + IMG_GRP * TXT, HD), BF16),
            pltpu.SemaphoreType.DMA((len(parts),)),
            pltpu.SemaphoreType.DMA((len(w_pieces),)),
        ],
        compiler_params=pltpu.CompilerParams(vmem_limit_bytes=60 << 20),
        name="attention",
    )((g // 8).reshape(1), txt_len, *parts, *w_parts, q_gain.reshape(1, HD), k_gain.reshape(1, HD), text_kv)

    from_up = lax.ppermute(mixed[1], "uly", down)
    from_down = lax.ppermute(mixed[2], "uly", up)
    from_far = lax.ppermute(mixed[3], "uly", [(i, (i + 4) % members) for i in range(members)])
    keep, send = pl.pallas_call(
        functools.partial(out_kernel, offsets),
        out_shape=[jax.ShapeDtypeStruct((rows, width), F32), jax.ShapeDtypeStruct((rows, width), BF16)],
        in_specs=[SMEM] + [VMEM] * 4 + [HBM],
        out_specs=[VMEM] * 2,
        scratch_shapes=[
            pltpu.VMEM((chip, depth // 2), BF16),
            pltpu.VMEM((width, depth // 2), BF16),
            pltpu.SemaphoreType.DMA((8 * len(offsets),)),
        ],
        compiler_params=pltpu.CompilerParams(vmem_limit_bytes=60 << 20),
        name="out",
    )(jnp.stack([g // 8, u // 2]), mixed[0], from_up, from_down, from_far, out_rows)
    came = lax.ppermute(send, "uly", swap)
    return pl.pallas_call(
        gate_kernel,
        grid=(2,),
        out_shape=jax.ShapeDtypeStruct((rows, width), BF16),
        in_specs=[
            pl.BlockSpec((rows, width // 2), lambda n: (0, n)),
            pl.BlockSpec((rows, width // 2), lambda n: (0, n)),
            pl.BlockSpec((rows, LANES), lambda n: (0, width // LANES)),
            pl.BlockSpec((IMG_GRP, width // 2), lambda n: (0, 4 + n)),
        ],
        out_specs=pl.BlockSpec((rows, width // 2), lambda n: (0, n)),
        compiler_params=pltpu.CompilerParams(vmem_limit_bytes=24 << 20),
        name="gate",
    )(keep, came, hidden, mods)


def solution(mesh):
    return jax.shard_map(
        body,
        mesh=mesh,
        in_specs=(
            P(("grp", "uly"), None),
            P(("grp", "uly")),
            P(("grp", "uly")),
            P("grp"),
            P("grp"),
            P(),
            P("grp", "uly"),
            P(),
            P(),
            P("grp", None, "uly"),
            P(None, "grp"),
        ),
        out_specs=P(("grp", "uly"), None),
        check_vma=False,
    )
```

```python
import functools
import math

import jax
import jax.numpy as jnp
from jax import lax
from jax.experimental import pallas as pl
from jax.experimental.pallas import tpu as pltpu
from jax.sharding import PartitionSpec as P

HD = 128
TXT = 128
BLK = 8
IMG_GRP = 2
LANES = 128
BF16 = jnp.bfloat16
F32 = jnp.float32


def modulation(timestep, mod_weight):
    half = mod_weight.shape[0] // 2
    freqs = jnp.exp(-math.log(10000.0) * jnp.arange(half, dtype=F32) / half)
    angles = timestep.astype(F32)[:, None] * freqs[None, :]
    embedded = jnp.concatenate([jnp.cos(angles), jnp.sin(angles)], axis=1)
    active = jax.nn.silu(embedded).astype(BF16)
    return jnp.dot(active, mod_weight, preferred_element_type=F32)


def pack_kernel(image_ref, slot_ref, core_ref, tokens_hbm, out_w_hbm, out_hbm, half_hbm, *refs):
    tok_ref, buf_ref, half_ref, in_sem, out_sem, w_sem = refs
    rows, width = tok_ref.shape
    slots = buf_ref.shape[0]
    chunk = width // 3
    loads, weights = [], []
    for i in range(4):
        source = out_w_hbm.at[:, pl.ds(pl.multiple_of((2 * i + core_ref[0]) * 256, 256), 256)]
        weights.append(pltpu.make_async_copy(source, half_ref.at[:, pl.ds(i * 256, 256)], w_sem.at[i]))
    for i in range(3):
        part = pl.ds(i * chunk, chunk)
        loads.append(pltpu.make_async_copy(tokens_hbm.at[:, part], tok_ref.at[:, part], in_sem.at[i]))
    for copy in weights + loads:
        copy.start()
    for copy in weights:
        copy.wait()
    half_copy = pltpu.make_async_copy(half_ref, half_hbm, w_sem.at[4])
    half_copy.start()
    lane_block = lax.broadcasted_iota(jnp.int32, (slots, rows), 1) // BLK
    row_block = lax.broadcasted_iota(jnp.int32, (rows, LANES), 0) // BLK
    target = jnp.zeros((slots, rows), jnp.int32)
    tags = jnp.zeros((rows, LANES), jnp.int32)
    for b in range(rows // BLK):
        image = image_ref[b]
        group = image // IMG_GRP
        tag = slot_ref[b] + 16 * (image - IMG_GRP * group) + 1
        target = jnp.where(lane_block == b, group * BLK, target)
        tags = jnp.where(row_block == b, tag, tags)
    target = target + lax.broadcasted_iota(jnp.int32, (slots, rows), 1) % BLK
    place = (lax.broadcasted_iota(jnp.int32, (slots, rows), 0) == target).astype(F32).astype(BF16)
    stores = []
    for i in range(3):
        cols = slice(i * chunk, i * chunk + chunk)
        stop = i * chunk + chunk
        if i == 2:
            buf_ref[:, width:] = jnp.dot(place, tags.astype(F32).astype(BF16), preferred_element_type=F32).astype(BF16)
            stop = width + LANES
        loads[i].wait()
        buf_ref[:, cols] = jnp.dot(place, tok_ref[:, cols], preferred_element_type=F32).astype(BF16)
        part = pl.ds(i * chunk, stop - i * chunk)
        stores.append(pltpu.make_async_copy(buf_ref.at[:, part], out_hbm.at[:, part], out_sem.at[i]))
        stores[-1].start()
    for copy in stores + [half_copy]:
        copy.wait()


def norm_kernel(arrived_ref, mods_ref, out_ref, x_ref):
    slots = arrived_ref.shape[0]
    rows, width = x_ref.shape
    tags = arrived_ref[:, width:].astype(F32)
    lane_tag = tags.T.astype(jnp.int32)
    lane = lax.broadcasted_iota(jnp.int32, (rows, slots), 1)
    target = ((lane_tag - 1) % 16) * BLK + lane % BLK
    hit = (lax.broadcasted_iota(jnp.int32, (rows, slots), 0) == target) & (lane_tag > 0)
    place = hit.astype(F32).astype(BF16)
    for start in range(0, width, 512):
        cols = slice(start, start + 512)
        x_ref[:, cols] = jnp.dot(place, arrived_ref[:, cols], preferred_element_type=F32)
    placed_tag = jnp.dot(place, arrived_ref[:, width:], preferred_element_type=F32)
    owner = (placed_tag > 16.5).astype(F32)
    second = owner[:, :1] > 0.5
    values = x_ref[...]
    mean = jnp.mean(values, axis=-1, keepdims=True)
    centred = values - mean
    spread = jnp.mean(centred * centred, axis=-1, keepdims=True)
    scale_by = lax.rsqrt(spread + 1e-06)
    for start in range(0, width, 512):
        cols = slice(start, start + 512)
        s_cols = slice(width + start, width + start + 512)
        shift = jnp.where(second, mods_ref[1:2, cols], mods_ref[0:1, cols])
        scale = jnp.where(second, mods_ref[1:2, s_cols], mods_ref[0:1, s_cols])
        normed = (x_ref[:, cols] - mean) * scale_by
        out_ref[:, cols] = (normed * (1.0 + scale) + shift).astype(BF16)
    out_ref[:, width:] = owner.astype(BF16)


def rms(values, gain):
    return values * lax.rsqrt(jnp.mean(values * values, axis=-1, keepdims=True) + 1e-06) * gain


def attention_kernel(pieces, w_pieces, tile, x_axis_ref, len_ref, *refs):
    hidden_refs, refs = refs[: len(pieces)], refs[len(pieces) :]
    w_refs, refs = refs[: len(w_pieces)], refs[len(w_pieces) :]
    qg_ref, kg_ref, text_ref = refs[:3]
    out_refs = refs[3:7]
    x_ref, w_ref, q_ref, k_ref, v_ref, x_sem, w_sem = refs[7:]
    tokens, full = x_ref.shape
    width = w_ref.shape[0]
    heads = w_ref.shape[1] // (3 * HD)
    w_copies = []
    for i, (ref, (dx, start)) in enumerate(zip(w_refs, w_pieces)):
        row = pl.multiple_of((x_axis_ref[0] + dx) % 4 * (width // 4) + start, 16)
        w_copies.append(pltpu.make_async_copy(ref, w_ref.at[pl.ds(row, ref.shape[0])], w_sem.at[i]))
        w_copies[-1].start()
    copies = []
    for i, (ref, (start, size)) in enumerate(zip(hidden_refs, pieces)):
        copies.append(pltpu.make_async_copy(ref, x_ref.at[pl.ds(start, size)], x_sem.at[i]))
        copies[-1].start()
    q_gain = qg_ref[...]
    k_gain = kg_ref[...]
    for h in range(heads):
        for i in range(IMG_GRP):
            at = tokens + i * TXT
            key = text_ref[i, :, 2 * h * HD : (2 * h + 1) * HD].astype(F32)
            k_ref[h, at : at + TXT, :] = rms(key, k_gain).astype(BF16)
            v_ref[h, at : at + TXT, :] = text_ref[i, :, (2 * h + 1) * HD : (2 * h + 2) * HD]
    for copy in w_copies:
        copy.wait()
    for start in range(0, tokens, 512):
        rows = slice(start, start + 512)
        for copy, (at, size) in zip(copies, pieces):
            if start <= at < start + 512:
                copy.wait()
        proj = jnp.dot(x_ref[rows, :width], w_ref[...], preferred_element_type=F32)
        for h in range(heads):
            at = 3 * h * HD
            q_ref[h, rows, :] = rms(proj[:, at : at + HD], q_gain).astype(BF16)
            k_ref[h, rows, :] = rms(proj[:, at + HD : at + 2 * HD], k_gain).astype(BF16)
            v_ref[h, rows, :] = proj[:, at + 2 * HD : at + 3 * HD].astype(BF16)
    lane = lax.broadcasted_iota(jnp.int32, (1, TXT), 1)
    codes = []
    for start in range(0, tokens, LANES):
        codes.append(x_ref[start : start + LANES, width:].astype(F32).T[:1])
    for i in range(IMG_GRP):
        codes.append(jnp.where(lane < len_ref[i], float(i), 2.0))
    code = jnp.concatenate(codes, axis=1)
    for start in range(0, tokens, tile):
        rows = slice(start, start + tile)
        match = x_ref[rows, width : width + 1].astype(F32) == code
        for h in range(heads):
            scores = lax.dot_general(
                q_ref[h, rows, :], k_ref[h], (((1,), (1,)), ((), ())), preferred_element_type=F32
            )
            weights = jnp.where(match, jnp.exp2(scores * (HD ** -0.5 * math.log2(math.e))), 0.0)
            total = jnp.sum(weights, axis=1, keepdims=True)
            summed = jnp.dot(weights.astype(BF16), v_ref[h], preferred_element_type=F32)
            out_refs[start // tile][:, h * HD : (h + 1) * HD] = (summed / total).astype(BF16)


def load_kernel(offsets, me_ref, w_hbm, out_ref, sem):
    block = out_ref.shape[0] // (8 * len(offsets))
    copies = []
    for i, dx in enumerate(offsets):
        for z in range(8):
            row = pl.multiple_of(((me_ref[0] + dx) % 4 * 8 + z) * block, 16)
            source = w_hbm.at[pl.ds((z * len(offsets) + i) * block, block)]
            copies.append(pltpu.make_async_copy(source, out_ref.at[pl.ds(row, block)], sem.at[i * 8 + z]))
    for copy in copies:
        copy.start()
    for copy in copies:
        copy.wait()


def out_kernel(me_ref, own_ref, *refs):
    others, (w_ref, keep_ref, send_ref, m_ref) = refs[:3], refs[3:]
    half = keep_ref.shape[0]
    for ref, offset in zip((own_ref,) + others, (0, 1, 3, 2)):
        at = pl.multiple_of((me_ref[1] + offset) % 4 * 256, 256)
        m_ref[:, pl.ds(at, 256)] = ref[...]
    block = 512
    for start in range(0, w_ref.shape[0], block):
        cols = slice(start, start + block)
        total = lax.dot_general(m_ref[...], w_ref[cols, :], (((1,), (1,)), ((), ())), preferred_element_type=F32)
        keep_ref[:, cols] = total[:half]
        send_ref[:, cols] = total[half:].astype(BF16)


def gate_kernel(keep_ref, came_ref, owner_ref, gate_ref, out_ref):
    second = owner_ref[:, :1].astype(F32) > 0.5
    gate = jnp.where(second, gate_ref[1:2, :], gate_ref[0:1, :])
    out_ref[...] = (gate * (keep_ref[...] + came_ref[...].astype(F32))).astype(BF16)


VMEM = pl.BlockSpec(memory_space=pltpu.VMEM)
SMEM = pl.BlockSpec(memory_space=pltpu.SMEM)
HBM = pl.BlockSpec(memory_space=pltpu.HBM)


def body(tokens, block_image, dest_slot, timestep, txt_len, mod_weight, qkv_weight, q_gain, k_gain, text_kv, out_weight):
    groups = lax.axis_size("grp")
    members = lax.axis_size("uly")
    u = lax.axis_index("uly").astype(jnp.int32)
    core = u % 2
    g = lax.axis_index("grp").astype(jnp.int32)
    rows, width = tokens.shape
    heads = qkv_weight.shape[1] // (3 * HD)
    depth = out_weight.shape[0]
    group_tokens = rows * members

    w_rows, wide = qkv_weight.shape
    outgoing, out_half = pl.pallas_call(
        pack_kernel,
        out_shape=[
            jax.ShapeDtypeStruct((groups * BLK, width + LANES), BF16),
            jax.ShapeDtypeStruct((w_rows, depth // 2), BF16),
        ],
        in_specs=[SMEM, SMEM, SMEM, HBM, HBM],
        out_specs=[HBM, HBM],
        scratch_shapes=[
            pltpu.VMEM((rows, width), BF16),
            pltpu.VMEM((groups * BLK, width + LANES), BF16),
            pltpu.VMEM((w_rows, depth // 2), BF16),
            pltpu.SemaphoreType.DMA((3,)),
            pltpu.SemaphoreType.DMA((3,)),
            pltpu.SemaphoreType.DMA((5,)),
        ],
        compiler_params=pltpu.CompilerParams(vmem_limit_bytes=60 << 20),
        name="pack",
    )(block_image, dest_slot, core.reshape(1), tokens, out_weight.T)

    def shift(dx, dz):
        return [(x * 8 + z, (x + dx) % 4 * 8 + (z + dz) % 8) for x in range(4) for z in range(8)]

    z_groups = [[x * 8 + z for z in range(8)] for x in range(4)]
    z_line = lax.all_gather(qkv_weight, "grp", axis=0, tiled=True, axis_index_groups=z_groups)
    arrived = lax.all_to_all(outgoing, "grp", split_axis=0, concat_axis=0, tiled=True)
    offsets = (0, -1, -2, -3)
    x_line = jnp.concatenate(
        [out_half] + [lax.ppermute(out_half, "grp", shift(-dx, 0)) for dx in offsets[1:]], axis=0
    )
    out_rows = lax.all_gather(x_line, "grp", axis=0, tiled=True, axis_index_groups=z_groups)
    mods = modulation(timestep, mod_weight)
    hidden = pl.pallas_call(
        norm_kernel,
        out_shape=jax.ShapeDtypeStruct((rows, width + LANES), BF16),
        in_specs=[VMEM, VMEM],
        out_specs=VMEM,
        scratch_shapes=[pltpu.VMEM((rows, width), F32)],
        compiler_params=pltpu.CompilerParams(vmem_limit_bytes=24 << 20),
        cost_estimate=pl.CostEstimate(flops=69_000_000_000, bytes_accessed=2_000_000, transcendentals=0),
        name="norm",
    )(arrived, mods[:, : 2 * width])

    up = [(i, (i + 2) % members) for i in range(members)]
    down = [(i, (i - 2) % members) for i in range(members)]
    swap = [(i, i ^ 1) for i in range(members)]
    half_rows = rows // 2
    tie = lax.optimization_barrier
    x_below = lax.ppermute(z_line, "grp", shift(1, 0))
    x_above = lax.ppermute(z_line, "grp", shift(-1, 0))
    below = lax.ppermute(hidden, "uly", up)
    above = lax.ppermute(hidden, "uly", down)
    beside = lax.ppermute(hidden, "uly", swap)
    below, above, beside, x_below, x_above = tie((below, above, beside, x_below, x_above))
    far_a = lax.ppermute(below[:half_rows], "uly", up)
    far_b = lax.ppermute(above[half_rows:], "uly", down)
    below_s = lax.ppermute(below, "uly", swap)
    half_line = z_line.shape[0] // 2
    x_far_a = lax.ppermute(x_below[:half_line], "grp", shift(1, 0))
    x_far_b = lax.ppermute(x_above[half_line:], "grp", shift(-1, 0))
    far_a, far_b, below_s, above, x_far_a, x_far_b = tie((far_a, far_b, below_s, above, x_far_a, x_far_b))
    above_s = lax.ppermute(above, "uly", swap)
    far_as = lax.ppermute(far_a, "uly", swap)
    far_bs = lax.ppermute(far_b, "uly", swap)
    w_parts = [z_line, x_below, x_above, x_far_a, x_far_b]
    w_pieces = ((0, 0), (3, 0), (1, 0), (2, 0), (2, half_line))
    me = jnp.stack([g // 8, u // 2])
    parts = [hidden, beside, below, below_s, above, above_s, far_a, far_b, far_as, far_bs]
    pieces, at = [], 0
    for part in parts:
        pieces.append((at, part.shape[0]))
        at += part.shape[0]
    chip = 2 * rows
    mixed = pl.pallas_call(
        functools.partial(attention_kernel, tuple(pieces), w_pieces, chip),
        out_shape=[jax.ShapeDtypeStruct((chip, heads * HD), BF16)] * 4,
        in_specs=[SMEM, SMEM] + [HBM] * (len(parts) + len(w_parts)) + [VMEM, VMEM, VMEM],
        out_specs=[VMEM] * 4,
        scratch_shapes=[
            pltpu.VMEM((group_tokens, width + LANES), BF16),
            pltpu.VMEM((width, 3 * heads * HD), BF16),
            pltpu.VMEM((heads, group_tokens, HD), BF16),
            pltpu.VMEM((heads, group_tokens + IMG_GRP * TXT, HD), BF16),
            pltpu.VMEM((heads, group_tokens + IMG_GRP * TXT, HD), BF16),
            pltpu.SemaphoreType.DMA((len(parts),)),
            pltpu.SemaphoreType.DMA((len(w_pieces),)),
        ],
        compiler_params=pltpu.CompilerParams(vmem_limit_bytes=60 << 20),
        name="attention",
    )(me, txt_len, *parts, *w_parts, q_gain.reshape(1, HD), k_gain.reshape(1, HD), text_kv)

    from_up = lax.ppermute(mixed[1], "uly", down)
    from_down = lax.ppermute(mixed[2], "uly", up)
    from_far = lax.ppermute(mixed[3], "uly", [(i, (i + 4) % members) for i in range(members)])
    loaded = pl.pallas_call(
        functools.partial(load_kernel, offsets),
        out_shape=jax.ShapeDtypeStruct((width, depth // 2), BF16),
        in_specs=[SMEM, HBM],
        out_specs=HBM,
        scratch_shapes=[pltpu.SemaphoreType.DMA((8 * len(offsets),))],
        compiler_params=pltpu.CompilerParams(vmem_limit_bytes=8 << 20),
        name="load",
    )(me, out_rows)
    keep, send = pl.pallas_call(
        out_kernel,
        out_shape=[jax.ShapeDtypeStruct((rows, width), F32), jax.ShapeDtypeStruct((rows, width), BF16)],
        in_specs=[SMEM] + [VMEM] * 5,
        out_specs=[VMEM] * 2,
        scratch_shapes=[pltpu.VMEM((chip, depth // 2), BF16)],
        compiler_params=pltpu.CompilerParams(vmem_limit_bytes=24 << 20),
        name="out",
    )(me, mixed[0], from_up, from_down, from_far, loaded)
    came = lax.ppermute(send, "uly", swap)
    return pl.pallas_call(
        gate_kernel,
        grid=(2,),
        out_shape=jax.ShapeDtypeStruct((rows, width), BF16),
        in_specs=[
            pl.BlockSpec((rows, width // 2), lambda n: (0, n)),
            pl.BlockSpec((rows, width // 2), lambda n: (0, n)),
            pl.BlockSpec((rows, LANES), lambda n: (0, width // LANES)),
            pl.BlockSpec((IMG_GRP, width // 2), lambda n: (0, 4 + n)),
        ],
        out_specs=pl.BlockSpec((rows, width // 2), lambda n: (0, n)),
        compiler_params=pltpu.CompilerParams(vmem_limit_bytes=24 << 20),
        name="gate",
    )(keep, came, hidden, mods)


def solution(mesh):
    return jax.shard_map(
        body,
        mesh=mesh,
        in_specs=(
            P(("grp", "uly"), None),
            P(("grp", "uly")),
            P(("grp", "uly")),
            P("grp"),
            P("grp"),
            P(),
            P("grp", "uly"),
            P(),
            P(),
            P("grp", None, "uly"),
            P(None, "grp"),
        ),
        out_specs=P(("grp", "uly"), None),
        check_vma=False,
    )
```

```python
import functools
import math

import jax
import jax.numpy as jnp
from jax import lax
from jax.experimental import pallas as pl
from jax.experimental.pallas import tpu as pltpu
from jax.sharding import PartitionSpec as P

HD = 128
TXT = 128
BLK = 8
IMG_GRP = 2
LANES = 128
BF16 = jnp.bfloat16
F32 = jnp.float32


def modulation(timestep, mod_weight):
    half = mod_weight.shape[0] // 2
    freqs = jnp.exp(-math.log(10000.0) * jnp.arange(half, dtype=F32) / half)
    angles = timestep.astype(F32)[:, None] * freqs[None, :]
    embedded = jnp.concatenate([jnp.cos(angles), jnp.sin(angles)], axis=1)
    active = jax.nn.silu(embedded).astype(BF16)
    return jnp.dot(active, mod_weight, preferred_element_type=F32)


def pack_kernel(image_ref, slot_ref, core_ref, tokens_hbm, out_w_hbm, out_hbm, half_hbm, *refs):
    tok_ref, buf_ref, half_ref, in_sem, out_sem, w_sem = refs
    rows, width = tok_ref.shape
    slots = buf_ref.shape[0]
    chunk = width // 3
    loads, weights = [], []
    for i in range(4):
        source = out_w_hbm.at[:, pl.ds(pl.multiple_of((2 * i + core_ref[0]) * 256, 256), 256)]
        weights.append(pltpu.make_async_copy(source, half_ref.at[:, pl.ds(i * 256, 256)], w_sem.at[i]))
    for i in range(3):
        part = pl.ds(i * chunk, chunk)
        loads.append(pltpu.make_async_copy(tokens_hbm.at[:, part], tok_ref.at[:, part], in_sem.at[i]))
    for copy in loads + weights:
        copy.start()
    lane_block = lax.broadcasted_iota(jnp.int32, (slots, rows), 1) // BLK
    row_block = lax.broadcasted_iota(jnp.int32, (rows, LANES), 0) // BLK
    target = jnp.zeros((slots, rows), jnp.int32)
    tags = jnp.zeros((rows, LANES), jnp.int32)
    for b in range(rows // BLK):
        image = image_ref[b]
        group = image // IMG_GRP
        tag = slot_ref[b] + 16 * (image - IMG_GRP * group) + 1
        target = jnp.where(lane_block == b, group * BLK, target)
        tags = jnp.where(row_block == b, tag, tags)
    target = target + lax.broadcasted_iota(jnp.int32, (slots, rows), 1) % BLK
    place = (lax.broadcasted_iota(jnp.int32, (slots, rows), 0) == target).astype(F32).astype(BF16)
    stores = []
    for i in range(3):
        cols = slice(i * chunk, i * chunk + chunk)
        stop = i * chunk + chunk
        if i == 2:
            buf_ref[:, width:] = jnp.dot(place, tags.astype(F32).astype(BF16), preferred_element_type=F32).astype(BF16)
            stop = width + LANES
        loads[i].wait()
        buf_ref[:, cols] = jnp.dot(place, tok_ref[:, cols], preferred_element_type=F32).astype(BF16)
        part = pl.ds(i * chunk, stop - i * chunk)
        stores.append(pltpu.make_async_copy(buf_ref.at[:, part], out_hbm.at[:, part], out_sem.at[i]))
        stores[-1].start()
    for copy in weights:
        copy.wait()
    half_copy = pltpu.make_async_copy(half_ref, half_hbm, w_sem.at[4])
    half_copy.start()
    for copy in stores + [half_copy]:
        copy.wait()


def norm_kernel(arrived_ref, mods_ref, out_ref, x_ref):
    slots = arrived_ref.shape[0]
    rows, width = x_ref.shape
    tags = arrived_ref[:, width:].astype(F32)
    lane_tag = tags.T.astype(jnp.int32)
    lane = lax.broadcasted_iota(jnp.int32, (rows, slots), 1)
    target = ((lane_tag - 1) % 16) * BLK + lane % BLK
    hit = (lax.broadcasted_iota(jnp.int32, (rows, slots), 0) == target) & (lane_tag > 0)
    place = hit.astype(F32).astype(BF16)
    for start in range(0, width, 512):
        cols = slice(start, start + 512)
        x_ref[:, cols] = jnp.dot(place, arrived_ref[:, cols], preferred_element_type=F32)
    placed_tag = jnp.dot(place, arrived_ref[:, width:], preferred_element_type=F32)
    owner = (placed_tag > 16.5).astype(F32)
    second = owner[:, :1] > 0.5
    values = x_ref[...]
    mean = jnp.mean(values, axis=-1, keepdims=True)
    centred = values - mean
    spread = jnp.mean(centred * centred, axis=-1, keepdims=True)
    scale_by = lax.rsqrt(spread + 1e-06)
    for start in range(0, width, 512):
        cols = slice(start, start + 512)
        s_cols = slice(width + start, width + start + 512)
        shift = jnp.where(second, mods_ref[1:2, cols], mods_ref[0:1, cols])
        scale = jnp.where(second, mods_ref[1:2, s_cols], mods_ref[0:1, s_cols])
        normed = (x_ref[:, cols] - mean) * scale_by
        out_ref[:, cols] = (normed * (1.0 + scale) + shift).astype(BF16)
    out_ref[:, width:] = owner.astype(BF16)


def rms(values, gain):
    return values * lax.rsqrt(jnp.mean(values * values, axis=-1, keepdims=True) + 1e-06) * gain


def attention_kernel(pieces, w_pieces, tile, x_axis_ref, len_ref, *refs):
    hidden_refs, refs = refs[: len(pieces)], refs[len(pieces) :]
    w_refs, refs = refs[: len(w_pieces)], refs[len(w_pieces) :]
    qg_ref, kg_ref, text_ref = refs[:3]
    out_refs = refs[3:7]
    x_ref, w_ref, q_ref, k_ref, v_ref, x_sem, w_sem = refs[7:]
    tokens, full = x_ref.shape
    width = w_ref.shape[0]
    heads = w_ref.shape[1] // (3 * HD)
    w_copies = []
    for i, (ref, (dx, start)) in enumerate(zip(w_refs, w_pieces)):
        row = pl.multiple_of((x_axis_ref[0] + dx) % 4 * (width // 4) + start, 16)
        w_copies.append(pltpu.make_async_copy(ref, w_ref.at[pl.ds(row, ref.shape[0])], w_sem.at[i]))
        w_copies[-1].start()
    copies = []
    for i, (ref, (start, size)) in enumerate(zip(hidden_refs, pieces)):
        copies.append(pltpu.make_async_copy(ref, x_ref.at[pl.ds(start, size)], x_sem.at[i]))
        copies[-1].start()
    q_gain = qg_ref[...]
    k_gain = kg_ref[...]
    for h in range(heads):
        for i in range(IMG_GRP):
            at = tokens + i * TXT
            key = text_ref[i, :, 2 * h * HD : (2 * h + 1) * HD].astype(F32)
            k_ref[h, at : at + TXT, :] = rms(key, k_gain).astype(BF16)
            v_ref[h, at : at + TXT, :] = text_ref[i, :, (2 * h + 1) * HD : (2 * h + 2) * HD]
    for copy in w_copies:
        copy.wait()
    for start in range(0, tokens, 512):
        rows = slice(start, start + 512)
        for copy, (at, size) in zip(copies, pieces):
            if start <= at < start + 512:
                copy.wait()
        proj = jnp.dot(x_ref[rows, :width], w_ref[...], preferred_element_type=F32)
        for h in range(heads):
            at = 3 * h * HD
            q_ref[h, rows, :] = rms(proj[:, at : at + HD], q_gain).astype(BF16)
            k_ref[h, rows, :] = rms(proj[:, at + HD : at + 2 * HD], k_gain).astype(BF16)
            v_ref[h, rows, :] = proj[:, at + 2 * HD : at + 3 * HD].astype(BF16)
    lane = lax.broadcasted_iota(jnp.int32, (1, TXT), 1)
    codes = []
    for start in range(0, tokens, LANES):
        codes.append(x_ref[start : start + LANES, width:].astype(F32).T[:1])
    for i in range(IMG_GRP):
        codes.append(jnp.where(lane < len_ref[i], float(i), 2.0))
    code = jnp.concatenate(codes, axis=1)
    for start in range(0, tokens, tile):
        rows = slice(start, start + tile)
        match = x_ref[rows, width : width + 1].astype(F32) == code
        for h in range(heads):
            scores = lax.dot_general(
                q_ref[h, rows, :], k_ref[h], (((1,), (1,)), ((), ())), preferred_element_type=F32
            )
            weights = jnp.where(match, jnp.exp2(scores * (HD ** -0.5 * math.log2(math.e))), 0.0)
            total = jnp.sum(weights, axis=1, keepdims=True)
            summed = jnp.dot(weights.astype(BF16), v_ref[h], preferred_element_type=F32)
            out_refs[start // tile][:, h * HD : (h + 1) * HD] = (summed / total).astype(BF16)


def out_kernel(offsets, me_ref, own_ref, *refs):
    others, (w_ref, keep_ref, send_ref, m_ref) = refs[:3], refs[3:]
    half = keep_ref.shape[0]
    part = w_ref.shape[0] // len(offsets)
    block = part // 8
    for ref, offset in zip((own_ref,) + others, (0, 1, 3, 2)):
        at = pl.multiple_of((me_ref[1] + offset) % 4 * 256, 256)
        m_ref[:, pl.ds(at, 256)] = ref[...]
    for i, dx in enumerate(offsets):
        starts = [(z * len(offsets) + i) * block for z in range(8)]
        rows = jnp.concatenate([w_ref[start : start + block, :] for start in starts], axis=0)
        total = lax.dot_general(m_ref[...], rows, (((1,), (1,)), ((), ())), preferred_element_type=F32)
        cols = pl.ds(pl.multiple_of((me_ref[0] + dx) % 4 * part, part), part)
        keep_ref[:, cols] = total[:half]
        send_ref[:, cols] = total[half:].astype(BF16)


def gate_kernel(keep_ref, came_ref, owner_ref, gate_ref, out_ref):
    second = owner_ref[:, :1].astype(F32) > 0.5
    gate = jnp.where(second, gate_ref[1:2, :], gate_ref[0:1, :])
    out_ref[...] = (gate * (keep_ref[...] + came_ref[...].astype(F32))).astype(BF16)


VMEM = pl.BlockSpec(memory_space=pltpu.VMEM)
SMEM = pl.BlockSpec(memory_space=pltpu.SMEM)
HBM = pl.BlockSpec(memory_space=pltpu.HBM)


def body(tokens, block_image, dest_slot, timestep, txt_len, mod_weight, qkv_weight, q_gain, k_gain, text_kv, out_weight):
    groups = lax.axis_size("grp")
    members = lax.axis_size("uly")
    u = lax.axis_index("uly").astype(jnp.int32)
    core = u % 2
    g = lax.axis_index("grp").astype(jnp.int32)
    rows, width = tokens.shape
    heads = qkv_weight.shape[1] // (3 * HD)
    depth = out_weight.shape[0]
    group_tokens = rows * members

    w_rows, wide = qkv_weight.shape
    outgoing, out_half = pl.pallas_call(
        pack_kernel,
        out_shape=[
            jax.ShapeDtypeStruct((groups * BLK, width + LANES), BF16),
            jax.ShapeDtypeStruct((w_rows, depth // 2), BF16),
        ],
        in_specs=[SMEM, SMEM, SMEM, HBM, HBM],
        out_specs=[HBM, HBM],
        scratch_shapes=[
            pltpu.VMEM((rows, width), BF16),
            pltpu.VMEM((groups * BLK, width + LANES), BF16),
            pltpu.VMEM((w_rows, depth // 2), BF16),
            pltpu.SemaphoreType.DMA((3,)),
            pltpu.SemaphoreType.DMA((3,)),
            pltpu.SemaphoreType.DMA((5,)),
        ],
        compiler_params=pltpu.CompilerParams(vmem_limit_bytes=60 << 20),
        name="pack",
    )(block_image, dest_slot, core.reshape(1), tokens, out_weight.T)

    def shift(dx, dz):
        return [(x * 8 + z, (x + dx) % 4 * 8 + (z + dz) % 8) for x in range(4) for z in range(8)]

    z_groups = [[x * 8 + z for z in range(8)] for x in range(4)]
    z_line = lax.all_gather(qkv_weight, "grp", axis=0, tiled=True, axis_index_groups=z_groups)
    arrived = lax.all_to_all(outgoing, "grp", split_axis=0, concat_axis=0, tiled=True)
    offsets = (0, -1, -2, -3)
    x_line = jnp.concatenate(
        [out_half] + [lax.ppermute(out_half, "grp", shift(-dx, 0)) for dx in offsets[1:]], axis=0
    )
    out_rows = lax.all_gather(x_line, "grp", axis=0, tiled=True, axis_index_groups=z_groups)
    mods = modulation(timestep, mod_weight)
    hidden = pl.pallas_call(
        norm_kernel,
        out_shape=jax.ShapeDtypeStruct((rows, width + LANES), BF16),
        in_specs=[VMEM, VMEM],
        out_specs=VMEM,
        scratch_shapes=[pltpu.VMEM((rows, width), F32)],
        compiler_params=pltpu.CompilerParams(vmem_limit_bytes=24 << 20),
        cost_estimate=pl.CostEstimate(flops=66_000_000_000, bytes_accessed=2_000_000, transcendentals=0),
        name="norm",
    )(arrived, mods[:, : 2 * width])

    up = [(i, (i + 2) % members) for i in range(members)]
    down = [(i, (i - 2) % members) for i in range(members)]
    swap = [(i, i ^ 1) for i in range(members)]
    half_rows = rows // 2
    tie = lax.optimization_barrier
    x_below = lax.ppermute(z_line, "grp", shift(1, 0))
    x_above = lax.ppermute(z_line, "grp", shift(-1, 0))
    below = lax.ppermute(hidden, "uly", up)
    above = lax.ppermute(hidden, "uly", down)
    beside = lax.ppermute(hidden, "uly", swap)
    below, above, beside, x_below, x_above = tie((below, above, beside, x_below, x_above))
    far_a = lax.ppermute(below[:half_rows], "uly", up)
    far_b = lax.ppermute(above[half_rows:], "uly", down)
    below_s = lax.ppermute(below, "uly", swap)
    half_line = z_line.shape[0] // 2
    x_far_a = lax.ppermute(x_below[:half_line], "grp", shift(1, 0))
    x_far_b = lax.ppermute(x_above[half_line:], "grp", shift(-1, 0))
    far_a, far_b, below_s, above, x_far_a, x_far_b = tie((far_a, far_b, below_s, above, x_far_a, x_far_b))
    above_s = lax.ppermute(above, "uly", swap)
    far_as = lax.ppermute(far_a, "uly", swap)
    far_bs = lax.ppermute(far_b, "uly", swap)
    w_parts = [z_line, x_below, x_above, x_far_a, x_far_b]
    w_pieces = ((0, 0), (3, 0), (1, 0), (2, 0), (2, half_line))
    me = jnp.stack([g // 8, u // 2])
    parts = [hidden, beside, below, below_s, above, above_s, far_a, far_b, far_as, far_bs]
    pieces, at = [], 0
    for part in parts:
        pieces.append((at, part.shape[0]))
        at += part.shape[0]
    chip = 2 * rows
    mixed = pl.pallas_call(
        functools.partial(attention_kernel, tuple(pieces), w_pieces, chip),
        out_shape=[jax.ShapeDtypeStruct((chip, heads * HD), BF16)] * 4,
        in_specs=[SMEM, SMEM] + [HBM] * (len(parts) + len(w_parts)) + [VMEM, VMEM, VMEM],
        out_specs=[VMEM] * 4,
        scratch_shapes=[
            pltpu.VMEM((group_tokens, width + LANES), BF16),
            pltpu.VMEM((width, 3 * heads * HD), BF16),
            pltpu.VMEM((heads, group_tokens, HD), BF16),
            pltpu.VMEM((heads, group_tokens + IMG_GRP * TXT, HD), BF16),
            pltpu.VMEM((heads, group_tokens + IMG_GRP * TXT, HD), BF16),
            pltpu.SemaphoreType.DMA((len(parts),)),
            pltpu.SemaphoreType.DMA((len(w_pieces),)),
        ],
        compiler_params=pltpu.CompilerParams(vmem_limit_bytes=60 << 20),
        name="attention",
    )(me, txt_len, *parts, *w_parts, q_gain.reshape(1, HD), k_gain.reshape(1, HD), text_kv)

    from_up = lax.ppermute(mixed[1], "uly", down)
    from_down = lax.ppermute(mixed[2], "uly", up)
    from_far = lax.ppermute(mixed[3], "uly", [(i, (i + 4) % members) for i in range(members)])
    keep, send = pl.pallas_call(
        functools.partial(out_kernel, offsets),
        out_shape=[jax.ShapeDtypeStruct((rows, width), F32), jax.ShapeDtypeStruct((rows, width), BF16)],
        in_specs=[SMEM] + [VMEM] * 5,
        out_specs=[VMEM] * 2,
        scratch_shapes=[pltpu.VMEM((chip, depth // 2), BF16)],
        compiler_params=pltpu.CompilerParams(vmem_limit_bytes=24 << 20),
        name="out",
    )(me, mixed[0], from_up, from_down, from_far, out_rows)
    came = lax.ppermute(send, "uly", swap)
    return pl.pallas_call(
        gate_kernel,
        grid=(2,),
        out_shape=jax.ShapeDtypeStruct((rows, width), BF16),
        in_specs=[
            pl.BlockSpec((rows, width // 2), lambda n: (0, n)),
            pl.BlockSpec((rows, width // 2), lambda n: (0, n)),
            pl.BlockSpec((rows, LANES), lambda n: (0, width // LANES)),
            pl.BlockSpec((IMG_GRP, width // 2), lambda n: (0, 4 + n)),
        ],
        out_specs=pl.BlockSpec((rows, width // 2), lambda n: (0, n)),
        compiler_params=pltpu.CompilerParams(vmem_limit_bytes=24 << 20),
        name="gate",
    )(keep, came, hidden, mods)


def solution(mesh):
    return jax.shard_map(
        body,
        mesh=mesh,
        in_specs=(
            P(("grp", "uly"), None),
            P(("grp", "uly")),
            P(("grp", "uly")),
            P("grp"),
            P("grp"),
            P(),
            P("grp", "uly"),
            P(),
            P(),
            P("grp", None, "uly"),
            P(None, "grp"),
        ),
        out_specs=P(("grp", "uly"), None),
        check_vma=False,
    )
```

```python
import functools
import math

import jax
import jax.numpy as jnp
from jax import lax
from jax.experimental import pallas as pl
from jax.experimental.pallas import tpu as pltpu
from jax.sharding import PartitionSpec as P

HD = 128
TXT = 128
BLK = 8
IMG_GRP = 2
LANES = 128
BF16 = jnp.bfloat16
F32 = jnp.float32


def modulation(timestep, mod_weight):
    half = mod_weight.shape[0] // 2
    freqs = jnp.exp(-math.log(10000.0) * jnp.arange(half, dtype=F32) / half)
    angles = timestep.astype(F32)[:, None] * freqs[None, :]
    embedded = jnp.concatenate([jnp.cos(angles), jnp.sin(angles)], axis=1)
    active = jax.nn.silu(embedded).astype(BF16)
    return jnp.dot(active, mod_weight, preferred_element_type=F32)


def pack_kernel(image_ref, slot_ref, core_ref, tokens_hbm, out_w_hbm, out_hbm, half_hbm, *refs):
    tok_ref, buf_ref, half_ref, in_sem, out_sem, w_sem = refs
    rows, width = tok_ref.shape
    slots = buf_ref.shape[0]
    chunk = width // 3
    loads, weights = [], []
    for i in range(4):
        source = out_w_hbm.at[:, pl.ds(pl.multiple_of((2 * i + core_ref[0]) * 256, 256), 256)]
        weights.append(pltpu.make_async_copy(source, half_ref.at[:, pl.ds(i * 256, 256)], w_sem.at[i]))
    for i in range(3):
        part = pl.ds(i * chunk, chunk)
        loads.append(pltpu.make_async_copy(tokens_hbm.at[:, part], tok_ref.at[:, part], in_sem.at[i]))
    for copy in loads + weights:
        copy.start()
    lane_block = lax.broadcasted_iota(jnp.int32, (slots, rows), 1) // BLK
    row_block = lax.broadcasted_iota(jnp.int32, (rows, LANES), 0) // BLK
    target = jnp.zeros((slots, rows), jnp.int32)
    tags = jnp.zeros((rows, LANES), jnp.int32)
    for b in range(rows // BLK):
        image = image_ref[b]
        group = image // IMG_GRP
        tag = slot_ref[b] + 16 * (image - IMG_GRP * group) + 1
        target = jnp.where(lane_block == b, group * BLK, target)
        tags = jnp.where(row_block == b, tag, tags)
    target = target + lax.broadcasted_iota(jnp.int32, (slots, rows), 1) % BLK
    place = (lax.broadcasted_iota(jnp.int32, (slots, rows), 0) == target).astype(F32).astype(BF16)
    stores = []
    for i in range(3):
        cols = slice(i * chunk, i * chunk + chunk)
        stop = i * chunk + chunk
        if i == 2:
            buf_ref[:, width:] = jnp.dot(place, tags.astype(F32).astype(BF16), preferred_element_type=F32).astype(BF16)
            stop = width + LANES
        loads[i].wait()
        buf_ref[:, cols] = jnp.dot(place, tok_ref[:, cols], preferred_element_type=F32).astype(BF16)
        part = pl.ds(i * chunk, stop - i * chunk)
        stores.append(pltpu.make_async_copy(buf_ref.at[:, part], out_hbm.at[:, part], out_sem.at[i]))
        stores[-1].start()
    for copy in weights:
        copy.wait()
    half_copy = pltpu.make_async_copy(half_ref, half_hbm, w_sem.at[4])
    half_copy.start()
    for copy in stores + [half_copy]:
        copy.wait()


def norm_kernel(arrived_ref, mods_ref, out_ref, x_ref):
    slots = arrived_ref.shape[0]
    rows, width = x_ref.shape
    tags = arrived_ref[:, width:].astype(F32)
    lane_tag = tags.T.astype(jnp.int32)
    lane = lax.broadcasted_iota(jnp.int32, (rows, slots), 1)
    target = ((lane_tag - 1) % 16) * BLK + lane % BLK
    hit = (lax.broadcasted_iota(jnp.int32, (rows, slots), 0) == target) & (lane_tag > 0)
    place = hit.astype(F32).astype(BF16)
    for start in range(0, width, 512):
        cols = slice(start, start + 512)
        x_ref[:, cols] = jnp.dot(place, arrived_ref[:, cols], preferred_element_type=F32)
    placed_tag = jnp.dot(place, arrived_ref[:, width:], preferred_element_type=F32)
    owner = (placed_tag > 16.5).astype(F32)
    second = owner[:, :1] > 0.5
    values = x_ref[...]
    mean = jnp.mean(values, axis=-1, keepdims=True)
    centred = values - mean
    spread = jnp.mean(centred * centred, axis=-1, keepdims=True)
    scale_by = lax.rsqrt(spread + 1e-06)
    for start in range(0, width, 512):
        cols = slice(start, start + 512)
        s_cols = slice(width + start, width + start + 512)
        shift = jnp.where(second, mods_ref[1:2, cols], mods_ref[0:1, cols])
        scale = jnp.where(second, mods_ref[1:2, s_cols], mods_ref[0:1, s_cols])
        normed = (x_ref[:, cols] - mean) * scale_by
        out_ref[:, cols] = (normed * (1.0 + scale) + shift).astype(BF16)
    out_ref[:, width:] = owner.astype(BF16)


def rms(values, gain):
    return values * lax.rsqrt(jnp.mean(values * values, axis=-1, keepdims=True) + 1e-06) * gain


def attention_kernel(pieces, w_pieces, tile, me_ref, len_ref, *refs):
    hidden_refs, refs = refs[: len(pieces)], refs[len(pieces) :]
    w_refs, refs = refs[: len(w_pieces)], refs[len(w_pieces) :]
    qg_ref, kg_ref, text_hbm = refs[:3]
    out_refs = refs[3:7]
    x_ref, own_ref, w_ref, text_ref, sum_ref, q_ref, k_ref, v_ref, x_sem, own_sem, w_sem, text_sem = refs[7:]
    tokens, width = x_ref.shape
    heads = w_ref.shape[1] // (3 * HD)
    steps = list(dict.fromkeys(dx for dx, _ in w_pieces))
    span = width // len(steps)
    waits = []
    for step, dx in enumerate(steps):
        waits.append([])
        for i, (ref, (other, start)) in enumerate(zip(w_refs, w_pieces)):
            if other == dx:
                to = w_ref.at[pl.ds(step * span + start, ref.shape[0])]
                waits[step].append(pltpu.make_async_copy(ref, to, w_sem.at[i]))
        column = pl.multiple_of((me_ref[0] + dx) % 4 * span, LANES)
        for i, (ref, (start, size)) in enumerate(zip(hidden_refs, pieces)):
            to = x_ref.at[pl.ds(start, size), pl.ds(step * span, span)]
            number = step * len(pieces) + i
            waits[step].append(pltpu.make_async_copy(ref.at[:, pl.ds(column, span)], to, x_sem.at[number]))
        for copy in waits[step]:
            copy.start()
    text_copy = pltpu.make_async_copy(text_hbm, text_ref, text_sem)
    text_copy.start()
    owners = []
    for i, (ref, (start, size)) in enumerate(zip(hidden_refs, pieces)):
        owners.append(
            pltpu.make_async_copy(ref.at[:, pl.ds(width, LANES)], own_ref.at[pl.ds(start, size)], own_sem.at[i])
        )
        owners[-1].start()
    for step in range(len(steps)):
        for copy in waits[step]:
            copy.wait()
        if step == len(steps) - 1:
            break
        inner = slice(step * span, step * span + span)
        for start in range(0, tokens, 512):
            rows = slice(start, start + 512)
            part = jnp.dot(x_ref[rows, inner], w_ref[inner, :], preferred_element_type=F32)
            sum_ref[rows, :] = part if step == 0 else sum_ref[rows, :] + part
    q_gain = qg_ref[...]
    k_gain = kg_ref[...]
    text_copy.wait()
    for copy in owners:
        copy.wait()
    for h in range(heads):
        for i in range(IMG_GRP):
            at = tokens + i * TXT
            key = text_ref[i, :, 2 * h * HD : (2 * h + 1) * HD].astype(F32)
            k_ref[h, at : at + TXT, :] = rms(key, k_gain).astype(BF16)
            v_ref[h, at : at + TXT, :] = text_ref[i, :, (2 * h + 1) * HD : (2 * h + 2) * HD]
    inner = slice(width - span, width)
    for start in range(0, tokens, 512):
        rows = slice(start, start + 512)
        proj = sum_ref[rows, :] + jnp.dot(x_ref[rows, inner], w_ref[inner, :], preferred_element_type=F32)
        for h in range(heads):
            at = 3 * h * HD
            q_ref[h, rows, :] = rms(proj[:, at : at + HD], q_gain).astype(BF16)
            k_ref[h, rows, :] = rms(proj[:, at + HD : at + 2 * HD], k_gain).astype(BF16)
            v_ref[h, rows, :] = proj[:, at + 2 * HD : at + 3 * HD].astype(BF16)
    lane = lax.broadcasted_iota(jnp.int32, (1, TXT), 1)
    codes = []
    for start in range(0, tokens, LANES):
        codes.append(own_ref[start : start + LANES, :].astype(F32).T[:1])
    for i in range(IMG_GRP):
        codes.append(jnp.where(lane < len_ref[i], float(i), 2.0))
    code = jnp.concatenate(codes, axis=1)
    for start in range(0, tokens, tile):
        rows = slice(start, start + tile)
        match = own_ref[rows, :1].astype(F32) == code
        for h in range(heads):
            scores = lax.dot_general(
                q_ref[h, rows, :], k_ref[h], (((1,), (1,)), ((), ())), preferred_element_type=F32
            )
            weights = jnp.where(match, jnp.exp2(scores * (HD ** -0.5 * math.log2(math.e))), 0.0)
            total = jnp.sum(weights, axis=1, keepdims=True)
            summed = jnp.dot(weights.astype(BF16), v_ref[h], preferred_element_type=F32)
            out_refs[start // tile][:, h * HD : (h + 1) * HD] = (summed / total).astype(BF16)


def out_kernel(offsets, me_ref, own_ref, *refs):
    others, (w_ref, keep_ref, send_ref, m_ref) = refs[:3], refs[3:]
    half = keep_ref.shape[0]
    part = w_ref.shape[0] // len(offsets)
    block = part // 8
    for ref, offset in zip((own_ref,) + others, (0, 1, 3, 2)):
        at = pl.multiple_of((me_ref[1] + offset) % 4 * 256, 256)
        m_ref[:, pl.ds(at, 256)] = ref[...]
    for i, dx in enumerate(offsets):
        starts = [(z * len(offsets) + i) * block for z in range(8)]
        rows = jnp.concatenate([w_ref[start : start + block, :] for start in starts], axis=0)
        total = lax.dot_general(m_ref[...], rows, (((1,), (1,)), ((), ())), preferred_element_type=F32)
        cols = pl.ds(pl.multiple_of((me_ref[0] + dx) % 4 * part, part), part)
        keep_ref[:, cols] = total[:half]
        send_ref[:, cols] = total[half:].astype(BF16)


def gate_kernel(keep_ref, came_ref, owner_ref, gate_ref, out_ref):
    second = owner_ref[:, :1].astype(F32) > 0.5
    gate = jnp.where(second, gate_ref[1:2, :], gate_ref[0:1, :])
    out_ref[...] = (gate * (keep_ref[...] + came_ref[...].astype(F32))).astype(BF16)


VMEM = pl.BlockSpec(memory_space=pltpu.VMEM)
SMEM = pl.BlockSpec(memory_space=pltpu.SMEM)
HBM = pl.BlockSpec(memory_space=pltpu.HBM)


def body(tokens, block_image, dest_slot, timestep, txt_len, mod_weight, qkv_weight, q_gain, k_gain, text_kv, out_weight):
    groups = lax.axis_size("grp")
    members = lax.axis_size("uly")
    u = lax.axis_index("uly").astype(jnp.int32)
    core = u % 2
    g = lax.axis_index("grp").astype(jnp.int32)
    rows, width = tokens.shape
    heads = qkv_weight.shape[1] // (3 * HD)
    depth = out_weight.shape[0]
    group_tokens = rows * members

    w_rows, wide = qkv_weight.shape
    outgoing, out_half = pl.pallas_call(
        pack_kernel,
        out_shape=[
            jax.ShapeDtypeStruct((groups * BLK, width + LANES), BF16),
            jax.ShapeDtypeStruct((w_rows, depth // 2), BF16),
        ],
        in_specs=[SMEM, SMEM, SMEM, HBM, HBM],
        out_specs=[HBM, HBM],
        scratch_shapes=[
            pltpu.VMEM((rows, width), BF16),
            pltpu.VMEM((groups * BLK, width + LANES), BF16),
            pltpu.VMEM((w_rows, depth // 2), BF16),
            pltpu.SemaphoreType.DMA((3,)),
            pltpu.SemaphoreType.DMA((3,)),
            pltpu.SemaphoreType.DMA((5,)),
        ],
        compiler_params=pltpu.CompilerParams(vmem_limit_bytes=60 << 20),
        name="pack",
    )(block_image, dest_slot, core.reshape(1), tokens, out_weight.T)

    def shift(dx, dz):
        return [(x * 8 + z, (x + dx) % 4 * 8 + (z + dz) % 8) for x in range(4) for z in range(8)]

    z_groups = [[x * 8 + z for z in range(8)] for x in range(4)]
    z_line = lax.all_gather(qkv_weight, "grp", axis=0, tiled=True, axis_index_groups=z_groups)
    arrived = lax.all_to_all(outgoing, "grp", split_axis=0, concat_axis=0, tiled=True)
    offsets = (0, -1, -2, -3)
    x_line = jnp.concatenate(
        [out_half] + [lax.ppermute(out_half, "grp", shift(-dx, 0)) for dx in offsets[1:]], axis=0
    )
    out_rows = lax.all_gather(x_line, "grp", axis=0, tiled=True, axis_index_groups=z_groups)
    mods = modulation(timestep, mod_weight)
    hidden = pl.pallas_call(
        norm_kernel,
        out_shape=jax.ShapeDtypeStruct((rows, width + LANES), BF16),
        in_specs=[VMEM, VMEM],
        out_specs=VMEM,
        scratch_shapes=[pltpu.VMEM((rows, width), F32)],
        compiler_params=pltpu.CompilerParams(vmem_limit_bytes=24 << 20),
        cost_estimate=pl.CostEstimate(flops=66_000_000_000, bytes_accessed=2_000_000, transcendentals=0),
        name="norm",
    )(arrived, mods[:, : 2 * width])

    up = [(i, (i + 2) % members) for i in range(members)]
    down = [(i, (i - 2) % members) for i in range(members)]
    swap = [(i, i ^ 1) for i in range(members)]
    half_rows = rows // 2
    tie = lax.optimization_barrier
    x_below = lax.ppermute(z_line, "grp", shift(1, 0))
    x_above = lax.ppermute(z_line, "grp", shift(-1, 0))
    below = lax.ppermute(hidden, "uly", up)
    above = lax.ppermute(hidden, "uly", down)
    beside = lax.ppermute(hidden, "uly", swap)
    below, above, beside, x_below, x_above = tie((below, above, beside, x_below, x_above))
    far_a = lax.ppermute(below[:half_rows], "uly", up)
    far_b = lax.ppermute(above[half_rows:], "uly", down)
    below_s = lax.ppermute(below, "uly", swap)
    half_line = z_line.shape[0] // 2
    x_far_a = lax.ppermute(x_below[:half_line], "grp", shift(1, 0))
    x_far_b = lax.ppermute(x_above[half_line:], "grp", shift(-1, 0))
    far_a, far_b, below_s, above, x_far_a, x_far_b = tie((far_a, far_b, below_s, above, x_far_a, x_far_b))
    above_s = lax.ppermute(above, "uly", swap)
    far_as = lax.ppermute(far_a, "uly", swap)
    far_bs = lax.ppermute(far_b, "uly", swap)
    w_parts = [z_line, x_below, x_above, x_far_a, x_far_b]
    w_pieces = ((0, 0), (3, 0), (1, 0), (2, 0), (2, half_line))
    me = jnp.stack([g // 8, u // 2])
    parts = [hidden, beside, below, below_s, above, above_s, far_a, far_b, far_as, far_bs]
    pieces, at = [], 0
    for part in parts:
        pieces.append((at, part.shape[0]))
        at += part.shape[0]
    chip = 2 * rows
    mixed = pl.pallas_call(
        functools.partial(attention_kernel, tuple(pieces), w_pieces, chip),
        out_shape=[jax.ShapeDtypeStruct((chip, heads * HD), BF16)] * 4,
        in_specs=[SMEM, SMEM] + [HBM] * (len(parts) + len(w_parts)) + [VMEM, VMEM, HBM],
        out_specs=[VMEM] * 4,
        scratch_shapes=[
            pltpu.VMEM((group_tokens, width), BF16),
            pltpu.VMEM((group_tokens, LANES), BF16),
            pltpu.VMEM((width, 3 * heads * HD), BF16),
            pltpu.VMEM(text_kv.shape, BF16),
            pltpu.VMEM((group_tokens, 3 * heads * HD), F32),
            pltpu.VMEM((heads, group_tokens, HD), BF16),
            pltpu.VMEM((heads, group_tokens + IMG_GRP * TXT, HD), BF16),
            pltpu.VMEM((heads, group_tokens + IMG_GRP * TXT, HD), BF16),
            pltpu.SemaphoreType.DMA((4 * len(parts),)),
            pltpu.SemaphoreType.DMA((len(parts),)),
            pltpu.SemaphoreType.DMA((len(w_pieces),)),
            pltpu.SemaphoreType.DMA,
        ],
        compiler_params=pltpu.CompilerParams(vmem_limit_bytes=60 << 20),
        name="attention",
    )(me, txt_len, *parts, *w_parts, q_gain.reshape(1, HD), k_gain.reshape(1, HD), text_kv)

    from_up = lax.ppermute(mixed[1], "uly", down)
    from_down = lax.ppermute(mixed[2], "uly", up)
    from_far = lax.ppermute(mixed[3], "uly", [(i, (i + 4) % members) for i in range(members)])
    keep, send = pl.pallas_call(
        functools.partial(out_kernel, offsets),
        out_shape=[jax.ShapeDtypeStruct((rows, width), F32), jax.ShapeDtypeStruct((rows, width), BF16)],
        in_specs=[SMEM] + [VMEM] * 5,
        out_specs=[VMEM] * 2,
        scratch_shapes=[pltpu.VMEM((chip, depth // 2), BF16)],
        compiler_params=pltpu.CompilerParams(vmem_limit_bytes=24 << 20),
        name="out",
    )(me, mixed[0], from_up, from_down, from_far, out_rows)
    came = lax.ppermute(send, "uly", swap)
    return pl.pallas_call(
        gate_kernel,
        grid=(2,),
        out_shape=jax.ShapeDtypeStruct((rows, width), BF16),
        in_specs=[
            pl.BlockSpec((rows, width // 2), lambda n: (0, n)),
            pl.BlockSpec((rows, width // 2), lambda n: (0, n)),
            pl.BlockSpec((rows, LANES), lambda n: (0, width // LANES)),
            pl.BlockSpec((IMG_GRP, width // 2), lambda n: (0, 4 + n)),
        ],
        out_specs=pl.BlockSpec((rows, width // 2), lambda n: (0, n)),
        compiler_params=pltpu.CompilerParams(vmem_limit_bytes=24 << 20),
        name="gate",
    )(keep, came, hidden, mods)


def solution(mesh):
    return jax.shard_map(
        body,
        mesh=mesh,
        in_specs=(
            P(("grp", "uly"), None),
            P(("grp", "uly")),
            P(("grp", "uly")),
            P("grp"),
            P("grp"),
            P(),
            P("grp", "uly"),
            P(),
            P(),
            P("grp", None, "uly"),
            P(None, "grp"),
        ),
        out_specs=P(("grp", "uly"), None),
        check_vma=False,
    )
```

```python
import functools
import math

import jax
import jax.numpy as jnp
from jax import lax
from jax.experimental import pallas as pl
from jax.experimental.pallas import tpu as pltpu
from jax.sharding import PartitionSpec as P

HD = 128
TXT = 128
BLK = 8
IMG_GRP = 2
LANES = 128
BF16 = jnp.bfloat16
F32 = jnp.float32


def modulation(timestep, mod_weight):
    half = mod_weight.shape[0] // 2
    freqs = jnp.exp(-math.log(10000.0) * jnp.arange(half, dtype=F32) / half)
    angles = timestep.astype(F32)[:, None] * freqs[None, :]
    embedded = jnp.concatenate([jnp.cos(angles), jnp.sin(angles)], axis=1)
    active = jax.nn.silu(embedded).astype(BF16)
    return jnp.dot(active, mod_weight, preferred_element_type=F32)


def pack_kernel(image_ref, slot_ref, core_ref, tokens_hbm, out_w_hbm, out_hbm, half_hbm, *refs):
    tok_ref, buf_ref, half_ref, in_sem, out_sem, w_sem = refs
    rows, width = tok_ref.shape
    slots = buf_ref.shape[0]
    chunk = width // 3
    loads, weights = [], []
    for i in range(4):
        source = out_w_hbm.at[:, pl.ds(pl.multiple_of((2 * i + core_ref[0]) * 256, 256), 256)]
        weights.append(pltpu.make_async_copy(source, half_ref.at[:, pl.ds(i * 256, 256)], w_sem.at[i]))
    for i in range(3):
        part = pl.ds(i * chunk, chunk)
        loads.append(pltpu.make_async_copy(tokens_hbm.at[:, part], tok_ref.at[:, part], in_sem.at[i]))
    for copy in loads + weights:
        copy.start()
    lane_block = lax.broadcasted_iota(jnp.int32, (slots, rows), 1) // BLK
    row_block = lax.broadcasted_iota(jnp.int32, (rows, LANES), 0) // BLK
    target = jnp.zeros((slots, rows), jnp.int32)
    tags = jnp.zeros((rows, LANES), jnp.int32)
    for b in range(rows // BLK):
        image = image_ref[b]
        group = image // IMG_GRP
        tag = slot_ref[b] + 16 * (image - IMG_GRP * group) + 1
        target = jnp.where(lane_block == b, group * BLK, target)
        tags = jnp.where(row_block == b, tag, tags)
    target = target + lax.broadcasted_iota(jnp.int32, (slots, rows), 1) % BLK
    place = (lax.broadcasted_iota(jnp.int32, (slots, rows), 0) == target).astype(F32).astype(BF16)
    stores = []
    for i in range(3):
        cols = slice(i * chunk, i * chunk + chunk)
        stop = i * chunk + chunk
        if i == 2:
            buf_ref[:, width:] = jnp.dot(place, tags.astype(F32).astype(BF16), preferred_element_type=F32).astype(BF16)
            stop = width + LANES
        loads[i].wait()
        buf_ref[:, cols] = jnp.dot(place, tok_ref[:, cols], preferred_element_type=F32).astype(BF16)
        part = pl.ds(i * chunk, stop - i * chunk)
        stores.append(pltpu.make_async_copy(buf_ref.at[:, part], out_hbm.at[:, part], out_sem.at[i]))
        stores[-1].start()
    for copy in weights:
        copy.wait()
    half_copy = pltpu.make_async_copy(half_ref, half_hbm, w_sem.at[4])
    half_copy.start()
    for copy in stores + [half_copy]:
        copy.wait()


def norm_kernel(arrived_ref, mods_ref, out_ref, x_ref):
    slots = arrived_ref.shape[0]
    rows, width = x_ref.shape
    tags = arrived_ref[:, width:].astype(F32)
    lane_tag = tags.T.astype(jnp.int32)
    lane = lax.broadcasted_iota(jnp.int32, (rows, slots), 1)
    target = ((lane_tag - 1) % 16) * BLK + lane % BLK
    hit = (lax.broadcasted_iota(jnp.int32, (rows, slots), 0) == target) & (lane_tag > 0)
    place = hit.astype(F32).astype(BF16)
    for start in range(0, width, 512):
        cols = slice(start, start + 512)
        x_ref[:, cols] = jnp.dot(place, arrived_ref[:, cols], preferred_element_type=F32)
    placed_tag = jnp.dot(place, arrived_ref[:, width:], preferred_element_type=F32)
    owner = (placed_tag > 16.5).astype(F32)
    second = owner[:, :1] > 0.5
    values = x_ref[...]
    mean = jnp.mean(values, axis=-1, keepdims=True)
    centred = values - mean
    spread = jnp.mean(centred * centred, axis=-1, keepdims=True)
    scale_by = lax.rsqrt(spread + 1e-06)
    for start in range(0, width, 512):
        cols = slice(start, start + 512)
        s_cols = slice(width + start, width + start + 512)
        shift = jnp.where(second, mods_ref[1:2, cols], mods_ref[0:1, cols])
        scale = jnp.where(second, mods_ref[1:2, s_cols], mods_ref[0:1, s_cols])
        normed = (x_ref[:, cols] - mean) * scale_by
        out_ref[:, cols] = (normed * (1.0 + scale) + shift).astype(BF16)
    out_ref[:, width:] = owner.astype(BF16)


def rms(values, gain):
    return values * lax.rsqrt(jnp.mean(values * values, axis=-1, keepdims=True) + 1e-06) * gain


def attention_kernel(pieces, w_pieces, tile, me_ref, len_ref, *refs):
    hidden_refs, refs = refs[: len(pieces)], refs[len(pieces) :]
    w_refs, refs = refs[: len(w_pieces)], refs[len(w_pieces) :]
    qg_ref, kg_ref, text_hbm = refs[:3]
    out_refs = refs[3:7]
    x_ref, own_ref, w_ref, text_ref, sum_ref, q_ref, k_ref, v_ref, x_sem, own_sem, w_sem, text_sem = refs[7:]
    tokens, width = x_ref.shape
    heads = w_ref.shape[1] // (3 * HD)
    steps = list(dict.fromkeys(dx for dx, _ in w_pieces))
    span = width // len(steps)
    waits = []
    for step, dx in enumerate(steps):
        waits.append([])
        for i, (ref, (other, start)) in enumerate(zip(w_refs, w_pieces)):
            if other == dx:
                to = w_ref.at[pl.ds(step * span + start, ref.shape[0])]
                waits[step].append(pltpu.make_async_copy(ref, to, w_sem.at[i]))
        column = pl.multiple_of((me_ref[0] + dx) % 4 * span, LANES)
        for i, (ref, (start, size)) in enumerate(zip(hidden_refs, pieces)):
            to = x_ref.at[pl.ds(start, size), pl.ds(step * span, span)]
            number = step * len(pieces) + i
            waits[step].append(pltpu.make_async_copy(ref.at[:, pl.ds(column, span)], to, x_sem.at[number]))
        for copy in waits[step]:
            copy.start()
    text_copy = pltpu.make_async_copy(text_hbm, text_ref, text_sem)
    text_copy.start()
    owners = []
    for i, (ref, (start, size)) in enumerate(zip(hidden_refs, pieces)):
        owners.append(
            pltpu.make_async_copy(ref.at[:, pl.ds(width, LANES)], own_ref.at[pl.ds(start, size)], own_sem.at[i])
        )
        owners[-1].start()
    for step in range(len(steps)):
        for copy in waits[step]:
            copy.wait()
        if step == len(steps) - 1:
            break
        inner = slice(step * span, step * span + span)
        for start in range(0, tokens, 512):
            rows = slice(start, start + 512)
            part = jnp.dot(x_ref[rows, inner], w_ref[inner, :], preferred_element_type=F32)
            sum_ref[rows, :] = part if step == 0 else sum_ref[rows, :] + part
    q_gain = qg_ref[...]
    k_gain = kg_ref[...]
    text_copy.wait()
    for copy in owners:
        copy.wait()
    for h in range(heads):
        for i in range(IMG_GRP):
            at = tokens + i * TXT
            key = text_ref[i, :, 2 * h * HD : (2 * h + 1) * HD].astype(F32)
            k_ref[h, at : at + TXT, :] = rms(key, k_gain).astype(BF16)
            v_ref[h, at : at + TXT, :] = text_ref[i, :, (2 * h + 1) * HD : (2 * h + 2) * HD]
    inner = slice(width - span, width)
    for start in range(0, tokens, 512):
        rows = slice(start, start + 512)
        proj = sum_ref[rows, :] + jnp.dot(x_ref[rows, inner], w_ref[inner, :], preferred_element_type=F32)
        for h in range(heads):
            at = 3 * h * HD
            q_ref[h, rows, :] = rms(proj[:, at : at + HD], q_gain).astype(BF16)
            k_ref[h, rows, :] = rms(proj[:, at + HD : at + 2 * HD], k_gain).astype(BF16)
            v_ref[h, rows, :] = proj[:, at + 2 * HD : at + 3 * HD].astype(BF16)
    lane = lax.broadcasted_iota(jnp.int32, (1, TXT), 1)
    codes = []
    for start in range(0, tokens, LANES):
        codes.append(own_ref[start : start + LANES, :].astype(F32).T[:1])
    for i in range(IMG_GRP):
        codes.append(jnp.where(lane < len_ref[i], float(i), 2.0))
    code = jnp.concatenate(codes, axis=1)
    for start in range(0, tokens, tile):
        rows = slice(start, start + tile)
        match = own_ref[rows, :1].astype(F32) == code
        for h in range(heads):
            scores = lax.dot_general(
                q_ref[h, rows, :], k_ref[h], (((1,), (1,)), ((), ())), preferred_element_type=F32
            )
            weights = jnp.where(match, jnp.exp2(scores * (HD ** -0.5 * math.log2(math.e))), 0.0)
            total = jnp.sum(weights, axis=1, keepdims=True)
            summed = jnp.dot(weights.astype(BF16), v_ref[h], preferred_element_type=F32)
            out_refs[start // tile][:, h * HD : (h + 1) * HD] = (summed / total).astype(BF16)


def out_kernel(offsets, me_ref, own_ref, *refs):
    others, (w_ref, keep_ref, send_ref, m_ref) = refs[:3], refs[3:]
    half = keep_ref.shape[0]
    part = w_ref.shape[0] // len(offsets)
    block = part // 8
    for ref, offset in zip((own_ref,) + others, (0, 1, 3, 2)):
        at = pl.multiple_of((me_ref[1] + offset) % 4 * 256, 256)
        m_ref[:, pl.ds(at, 256)] = ref[...]
    for i, dx in enumerate(offsets):
        starts = [(z * len(offsets) + i) * block for z in range(8)]
        rows = jnp.concatenate([w_ref[start : start + block, :] for start in starts], axis=0)
        total = lax.dot_general(m_ref[...], rows, (((1,), (1,)), ((), ())), preferred_element_type=F32)
        cols = pl.ds(pl.multiple_of((me_ref[0] + dx) % 4 * part, part), part)
        keep_ref[:, cols] = total[:half]
        send_ref[:, cols] = total[half:].astype(BF16)


def gate_kernel(keep_ref, came_ref, owner_ref, gate_ref, out_ref):
    second = owner_ref[:, :1].astype(F32) > 0.5
    gate = jnp.where(second, gate_ref[1:2, :], gate_ref[0:1, :])
    out_ref[...] = (gate * (keep_ref[...] + came_ref[...].astype(F32))).astype(BF16)


VMEM = pl.BlockSpec(memory_space=pltpu.VMEM)
SMEM = pl.BlockSpec(memory_space=pltpu.SMEM)
HBM = pl.BlockSpec(memory_space=pltpu.HBM)


def body(tokens, block_image, dest_slot, timestep, txt_len, mod_weight, qkv_weight, q_gain, k_gain, text_kv, out_weight):
    groups = lax.axis_size("grp")
    members = lax.axis_size("uly")
    u = lax.axis_index("uly").astype(jnp.int32)
    core = u % 2
    g = lax.axis_index("grp").astype(jnp.int32)
    rows, width = tokens.shape
    heads = qkv_weight.shape[1] // (3 * HD)
    depth = out_weight.shape[0]
    group_tokens = rows * members

    w_rows, wide = qkv_weight.shape
    outgoing, out_half = pl.pallas_call(
        pack_kernel,
        out_shape=[
            jax.ShapeDtypeStruct((groups * BLK, width + LANES), BF16),
            jax.ShapeDtypeStruct((w_rows, depth // 2), BF16),
        ],
        in_specs=[SMEM, SMEM, SMEM, HBM, HBM],
        out_specs=[HBM, HBM],
        scratch_shapes=[
            pltpu.VMEM((rows, width), BF16),
            pltpu.VMEM((groups * BLK, width + LANES), BF16),
            pltpu.VMEM((w_rows, depth // 2), BF16),
            pltpu.SemaphoreType.DMA((3,)),
            pltpu.SemaphoreType.DMA((3,)),
            pltpu.SemaphoreType.DMA((5,)),
        ],
        compiler_params=pltpu.CompilerParams(vmem_limit_bytes=60 << 20),
        name="pack",
    )(block_image, dest_slot, core.reshape(1), tokens, out_weight.T)

    def shift(dx, dz):
        return [(x * 8 + z, (x + dx) % 4 * 8 + (z + dz) % 8) for x in range(4) for z in range(8)]

    z_groups = [[x * 8 + z for z in range(8)] for x in range(4)]
    z_line = lax.all_gather(qkv_weight, "grp", axis=0, tiled=True, axis_index_groups=z_groups)
    arrived = lax.all_to_all(outgoing, "grp", split_axis=0, concat_axis=0, tiled=True)
    offsets = (0, -1, -2, -3)
    x_line = jnp.concatenate(
        [out_half] + [lax.ppermute(out_half, "grp", shift(-dx, 0)) for dx in offsets[1:]], axis=0
    )
    out_rows = lax.all_gather(x_line, "grp", axis=0, tiled=True, axis_index_groups=z_groups)
    mods = modulation(timestep, mod_weight)
    hidden = pl.pallas_call(
        norm_kernel,
        out_shape=jax.ShapeDtypeStruct((rows, width + LANES), BF16),
        in_specs=[VMEM, VMEM],
        out_specs=VMEM,
        scratch_shapes=[pltpu.VMEM((rows, width), F32)],
        compiler_params=pltpu.CompilerParams(vmem_limit_bytes=24 << 20),
        cost_estimate=pl.CostEstimate(flops=66_000_000_000, bytes_accessed=2_000_000, transcendentals=0),
        name="norm",
    )(arrived, mods[:, : 2 * width])

    up = [(i, (i + 2) % members) for i in range(members)]
    down = [(i, (i - 2) % members) for i in range(members)]
    swap = [(i, i ^ 1) for i in range(members)]
    half_rows = rows // 2
    tie = lax.optimization_barrier
    x_below = lax.ppermute(z_line, "grp", shift(1, 0))
    x_above = lax.ppermute(z_line, "grp", shift(-1, 0))
    below = lax.ppermute(hidden, "uly", up)
    above = lax.ppermute(hidden, "uly", down)
    beside = lax.ppermute(hidden, "uly", swap)
    below, above, beside = tie((below, above, beside))
    far_a = lax.ppermute(below[:half_rows], "uly", up)
    far_b = lax.ppermute(above[half_rows:], "uly", down)
    below_s = lax.ppermute(below, "uly", swap)
    half_line = z_line.shape[0] // 2
    x_far_a = lax.ppermute(x_below[:half_line], "grp", shift(1, 0))
    x_far_b = lax.ppermute(x_above[half_line:], "grp", shift(-1, 0))
    far_a, far_b, below_s, above, x_far_a, x_far_b = tie((far_a, far_b, below_s, above, x_far_a, x_far_b))
    above_s = lax.ppermute(above, "uly", swap)
    far_as = lax.ppermute(far_a, "uly", swap)
    far_bs = lax.ppermute(far_b, "uly", swap)
    w_parts = [z_line, x_below, x_above, x_far_a, x_far_b]
    w_pieces = ((0, 0), (3, 0), (1, 0), (2, 0), (2, half_line))
    me = jnp.stack([g // 8, u // 2])
    parts = [hidden, beside, below, below_s, above, above_s, far_a, far_b, far_as, far_bs]
    pieces, at = [], 0
    for part in parts:
        pieces.append((at, part.shape[0]))
        at += part.shape[0]
    chip = 2 * rows
    mixed = pl.pallas_call(
        functools.partial(attention_kernel, tuple(pieces), w_pieces, chip),
        out_shape=[jax.ShapeDtypeStruct((chip, heads * HD), BF16)] * 4,
        in_specs=[SMEM, SMEM] + [HBM] * (len(parts) + len(w_parts)) + [VMEM, VMEM, HBM],
        out_specs=[VMEM] * 4,
        scratch_shapes=[
            pltpu.VMEM((group_tokens, width), BF16),
            pltpu.VMEM((group_tokens, LANES), BF16),
            pltpu.VMEM((width, 3 * heads * HD), BF16),
            pltpu.VMEM(text_kv.shape, BF16),
            pltpu.VMEM((group_tokens, 3 * heads * HD), F32),
            pltpu.VMEM((heads, group_tokens, HD), BF16),
            pltpu.VMEM((heads, group_tokens + IMG_GRP * TXT, HD), BF16),
            pltpu.VMEM((heads, group_tokens + IMG_GRP * TXT, HD), BF16),
            pltpu.SemaphoreType.DMA((4 * len(parts),)),
            pltpu.SemaphoreType.DMA((len(parts),)),
            pltpu.SemaphoreType.DMA((len(w_pieces),)),
            pltpu.SemaphoreType.DMA,
        ],
        compiler_params=pltpu.CompilerParams(vmem_limit_bytes=60 << 20),
        name="attention",
    )(me, txt_len, *parts, *w_parts, q_gain.reshape(1, HD), k_gain.reshape(1, HD), text_kv)

    from_up = lax.ppermute(mixed[1], "uly", down)
    from_down = lax.ppermute(mixed[2], "uly", up)
    from_far = lax.ppermute(mixed[3], "uly", [(i, (i + 4) % members) for i in range(members)])
    keep, send = pl.pallas_call(
        functools.partial(out_kernel, offsets),
        out_shape=[jax.ShapeDtypeStruct((rows, width), F32), jax.ShapeDtypeStruct((rows, width), BF16)],
        in_specs=[SMEM] + [VMEM] * 5,
        out_specs=[VMEM] * 2,
        scratch_shapes=[pltpu.VMEM((chip, depth // 2), BF16)],
        compiler_params=pltpu.CompilerParams(vmem_limit_bytes=24 << 20),
        name="out",
    )(me, mixed[0], from_up, from_down, from_far, out_rows)
    came = lax.ppermute(send, "uly", swap)
    return pl.pallas_call(
        gate_kernel,
        grid=(2,),
        out_shape=jax.ShapeDtypeStruct((rows, width), BF16),
        in_specs=[
            pl.BlockSpec((rows, width // 2), lambda n: (0, n)),
            pl.BlockSpec((rows, width // 2), lambda n: (0, n)),
            pl.BlockSpec((rows, LANES), lambda n: (0, width // LANES)),
            pl.BlockSpec((IMG_GRP, width // 2), lambda n: (0, 4 + n)),
        ],
        out_specs=pl.BlockSpec((rows, width // 2), lambda n: (0, n)),
        compiler_params=pltpu.CompilerParams(vmem_limit_bytes=24 << 20),
        name="gate",
    )(keep, came, hidden, mods)


def solution(mesh):
    return jax.shard_map(
        body,
        mesh=mesh,
        in_specs=(
            P(("grp", "uly"), None),
            P(("grp", "uly")),
            P(("grp", "uly")),
            P("grp"),
            P("grp"),
            P(),
            P("grp", "uly"),
            P(),
            P(),
            P("grp", None, "uly"),
            P(None, "grp"),
        ),
        out_specs=P(("grp", "uly"), None),
        check_vma=False,
    )
```

```python
import functools
import math

import jax
import jax.numpy as jnp
from jax import lax
from jax.experimental import pallas as pl
from jax.experimental.pallas import tpu as pltpu
from jax.sharding import PartitionSpec as P

HD = 128
TXT = 128
BLK = 8
IMG_GRP = 2
LANES = 128
BF16 = jnp.bfloat16
F32 = jnp.float32


def modulation(timestep, mod_weight):
    half = mod_weight.shape[0] // 2
    freqs = jnp.exp(-math.log(10000.0) * jnp.arange(half, dtype=F32) / half)
    angles = timestep.astype(F32)[:, None] * freqs[None, :]
    embedded = jnp.concatenate([jnp.cos(angles), jnp.sin(angles)], axis=1)
    active = jax.nn.silu(embedded).astype(BF16)
    return jnp.dot(active, mod_weight, preferred_element_type=F32)


def pack_kernel(image_ref, slot_ref, core_ref, tokens_hbm, out_w_hbm, out_hbm, half_hbm, *refs):
    tok_ref, buf_ref, half_ref, in_sem, out_sem, w_sem = refs
    rows, width = tok_ref.shape
    slots = buf_ref.shape[0]
    chunk = width // 3
    loads, weights = [], []
    for i in range(4):
        source = out_w_hbm.at[:, pl.ds(pl.multiple_of((2 * i + core_ref[0]) * 256, 256), 256)]
        weights.append(pltpu.make_async_copy(source, half_ref.at[:, pl.ds(i * 256, 256)], w_sem.at[i]))
    for i in range(3):
        part = pl.ds(i * chunk, chunk)
        loads.append(pltpu.make_async_copy(tokens_hbm.at[:, part], tok_ref.at[:, part], in_sem.at[i]))
    for copy in loads + weights:
        copy.start()
    lane_block = lax.broadcasted_iota(jnp.int32, (slots, rows), 1) // BLK
    row_block = lax.broadcasted_iota(jnp.int32, (rows, LANES), 0) // BLK
    target = jnp.zeros((slots, rows), jnp.int32)
    tags = jnp.zeros((rows, LANES), jnp.int32)
    for b in range(rows // BLK):
        image = image_ref[b]
        group = image // IMG_GRP
        tag = slot_ref[b] + 16 * (image - IMG_GRP * group) + 1
        target = jnp.where(lane_block == b, group * BLK, target)
        tags = jnp.where(row_block == b, tag, tags)
    target = target + lax.broadcasted_iota(jnp.int32, (slots, rows), 1) % BLK
    place = (lax.broadcasted_iota(jnp.int32, (slots, rows), 0) == target).astype(F32).astype(BF16)
    stores = []
    for i in range(3):
        cols = slice(i * chunk, i * chunk + chunk)
        stop = i * chunk + chunk
        if i == 2:
            buf_ref[:, width:] = jnp.dot(place, tags.astype(F32).astype(BF16), preferred_element_type=F32).astype(BF16)
            stop = width + LANES
        loads[i].wait()
        buf_ref[:, cols] = jnp.dot(place, tok_ref[:, cols], preferred_element_type=F32).astype(BF16)
        part = pl.ds(i * chunk, stop - i * chunk)
        stores.append(pltpu.make_async_copy(buf_ref.at[:, part], out_hbm.at[:, part], out_sem.at[i]))
        stores[-1].start()
    for copy in weights:
        copy.wait()
    half_copy = pltpu.make_async_copy(half_ref, half_hbm, w_sem.at[4])
    half_copy.start()
    for copy in stores + [half_copy]:
        copy.wait()


def norm_kernel(arrived_ref, mods_ref, out_ref, x_ref):
    slots = arrived_ref.shape[0]
    rows, width = x_ref.shape
    tags = arrived_ref[:, width:].astype(F32)
    lane_tag = tags.T.astype(jnp.int32)
    lane = lax.broadcasted_iota(jnp.int32, (rows, slots), 1)
    target = ((lane_tag - 1) % 16) * BLK + lane % BLK
    hit = (lax.broadcasted_iota(jnp.int32, (rows, slots), 0) == target) & (lane_tag > 0)
    place = hit.astype(F32).astype(BF16)
    for start in range(0, width, 512):
        cols = slice(start, start + 512)
        x_ref[:, cols] = jnp.dot(place, arrived_ref[:, cols], preferred_element_type=F32)
    placed_tag = jnp.dot(place, arrived_ref[:, width:], preferred_element_type=F32)
    owner = (placed_tag > 16.5).astype(F32)
    second = owner[:, :1] > 0.5
    values = x_ref[...]
    mean = jnp.mean(values, axis=-1, keepdims=True)
    centred = values - mean
    spread = jnp.mean(centred * centred, axis=-1, keepdims=True)
    scale_by = lax.rsqrt(spread + 1e-06)
    for start in range(0, width, 512):
        cols = slice(start, start + 512)
        s_cols = slice(width + start, width + start + 512)
        shift = jnp.where(second, mods_ref[1:2, cols], mods_ref[0:1, cols])
        scale = jnp.where(second, mods_ref[1:2, s_cols], mods_ref[0:1, s_cols])
        normed = (x_ref[:, cols] - mean) * scale_by
        out_ref[:, cols] = (normed * (1.0 + scale) + shift).astype(BF16)
    out_ref[:, width:] = owner.astype(BF16)


def rms(values, gain):
    return values * lax.rsqrt(jnp.mean(values * values, axis=-1, keepdims=True) + 1e-06) * gain


def attention_kernel(pieces, w_pieces, tile, me_ref, len_ref, *refs):
    hidden_refs, refs = refs[: len(pieces)], refs[len(pieces) :]
    w_refs, refs = refs[: len(w_pieces)], refs[len(w_pieces) :]
    qg_ref, kg_ref, text_hbm = refs[:3]
    out_refs = refs[3:7]
    x_ref, own_ref, w_ref, text_ref, sum_ref, q_ref, k_ref, v_ref, x_sem, own_sem, w_sem, text_sem = refs[7:]
    tokens, width = x_ref.shape
    heads = w_ref.shape[1] // (3 * HD)
    steps = list(dict.fromkeys(dx for dx, _ in w_pieces))
    span = width // len(steps)
    waits = []
    for step, dx in enumerate(steps):
        waits.append([])
        for i, (ref, (other, start)) in enumerate(zip(w_refs, w_pieces)):
            if other == dx:
                to = w_ref.at[pl.ds(step * span + start, ref.shape[0])]
                waits[step].append(pltpu.make_async_copy(ref, to, w_sem.at[i]))
        column = pl.multiple_of((me_ref[0] + dx) % 4 * span, LANES)
        for i, (ref, (start, size)) in enumerate(zip(hidden_refs, pieces)):
            to = x_ref.at[pl.ds(start, size), pl.ds(step * span, span)]
            number = step * len(pieces) + i
            waits[step].append(pltpu.make_async_copy(ref.at[:, pl.ds(column, span)], to, x_sem.at[number]))
        for copy in waits[step]:
            copy.start()
    text_copy = pltpu.make_async_copy(text_hbm, text_ref, text_sem)
    text_copy.start()
    owners = []
    for i, (ref, (start, size)) in enumerate(zip(hidden_refs, pieces)):
        owners.append(
            pltpu.make_async_copy(ref.at[:, pl.ds(width, LANES)], own_ref.at[pl.ds(start, size)], own_sem.at[i])
        )
        owners[-1].start()
    for step in range(len(steps)):
        for copy in waits[step]:
            copy.wait()
        if step == len(steps) - 1:
            break
        inner = slice(step * span, step * span + span)
        for start in range(0, tokens, 512):
            rows = slice(start, start + 512)
            part = jnp.dot(x_ref[rows, inner], w_ref[inner, :], preferred_element_type=F32)
            sum_ref[rows, :] = part if step == 0 else sum_ref[rows, :] + part
    q_gain = qg_ref[...]
    k_gain = kg_ref[...]
    text_copy.wait()
    for copy in owners:
        copy.wait()
    for h in range(heads):
        for i in range(IMG_GRP):
            at = tokens + i * TXT
            key = text_ref[i, :, 2 * h * HD : (2 * h + 1) * HD].astype(F32)
            k_ref[h, at : at + TXT, :] = rms(key, k_gain).astype(BF16)
            v_ref[h, at : at + TXT, :] = text_ref[i, :, (2 * h + 1) * HD : (2 * h + 2) * HD]
    inner = slice(width - span, width)
    for start in range(0, tokens, 512):
        rows = slice(start, start + 512)
        proj = sum_ref[rows, :] + jnp.dot(x_ref[rows, inner], w_ref[inner, :], preferred_element_type=F32)
        for h in range(heads):
            at = 3 * h * HD
            q_ref[h, rows, :] = rms(proj[:, at : at + HD], q_gain).astype(BF16)
            k_ref[h, rows, :] = rms(proj[:, at + HD : at + 2 * HD], k_gain).astype(BF16)
            v_ref[h, rows, :] = proj[:, at + 2 * HD : at + 3 * HD].astype(BF16)
    lane = lax.broadcasted_iota(jnp.int32, (1, TXT), 1)
    codes = []
    for start in range(0, tokens, LANES):
        codes.append(own_ref[start : start + LANES, :].astype(F32).T[:1])
    for i in range(IMG_GRP):
        codes.append(jnp.where(lane < len_ref[i], float(i), 2.0))
    code = jnp.concatenate(codes, axis=1)
    for start in range(0, tokens, tile):
        rows = slice(start, start + tile)
        match = own_ref[rows, :1].astype(F32) == code
        for h in range(heads):
            scores = lax.dot_general(
                q_ref[h, rows, :], k_ref[h], (((1,), (1,)), ((), ())), preferred_element_type=F32
            )
            weights = jnp.where(match, jnp.exp2(scores * (HD ** -0.5 * math.log2(math.e))), 0.0)
            total = jnp.sum(weights, axis=1, keepdims=True)
            summed = jnp.dot(weights.astype(BF16), v_ref[h], preferred_element_type=F32)
            out_refs[start // tile][:, h * HD : (h + 1) * HD] = (summed / total).astype(BF16)


def out_kernel(offsets, low, me_ref, own_ref, *refs):
    others, (w_ref, out_ref, m_ref) = refs[:3], refs[3:]
    half = out_ref.shape[0]
    part = w_ref.shape[0] // len(offsets)
    block = part // 8
    for ref, offset in zip((own_ref,) + others, (0, 1, 3, 2)):
        at = pl.multiple_of((me_ref[1] + offset) % 4 * 256, 256)
        m_ref[:, pl.ds(at, 256)] = ref[low : low + half, :]
    for i, dx in enumerate(offsets):
        starts = [(z * len(offsets) + i) * block for z in range(8)]
        rows = jnp.concatenate([w_ref[start : start + block, :] for start in starts], axis=0)
        total = lax.dot_general(m_ref[...], rows, (((1,), (1,)), ((), ())), preferred_element_type=F32)
        cols = pl.ds(pl.multiple_of((me_ref[0] + dx) % 4 * part, part), part)
        out_ref[:, cols] = total.astype(out_ref.dtype)


def gate_kernel(keep_ref, came_ref, owner_ref, gate_ref, out_ref):
    second = owner_ref[:, :1].astype(F32) > 0.5
    gate = jnp.where(second, gate_ref[1:2, :], gate_ref[0:1, :])
    out_ref[...] = (gate * (keep_ref[...] + came_ref[...].astype(F32))).astype(BF16)


VMEM = pl.BlockSpec(memory_space=pltpu.VMEM)
SMEM = pl.BlockSpec(memory_space=pltpu.SMEM)
HBM = pl.BlockSpec(memory_space=pltpu.HBM)


def body(tokens, block_image, dest_slot, timestep, txt_len, mod_weight, qkv_weight, q_gain, k_gain, text_kv, out_weight):
    groups = lax.axis_size("grp")
    members = lax.axis_size("uly")
    u = lax.axis_index("uly").astype(jnp.int32)
    core = u % 2
    g = lax.axis_index("grp").astype(jnp.int32)
    rows, width = tokens.shape
    heads = qkv_weight.shape[1] // (3 * HD)
    depth = out_weight.shape[0]
    group_tokens = rows * members

    w_rows, wide = qkv_weight.shape
    outgoing, out_half = pl.pallas_call(
        pack_kernel,
        out_shape=[
            jax.ShapeDtypeStruct((groups * BLK, width + LANES), BF16),
            jax.ShapeDtypeStruct((w_rows, depth // 2), BF16),
        ],
        in_specs=[SMEM, SMEM, SMEM, HBM, HBM],
        out_specs=[HBM, HBM],
        scratch_shapes=[
            pltpu.VMEM((rows, width), BF16),
            pltpu.VMEM((groups * BLK, width + LANES), BF16),
            pltpu.VMEM((w_rows, depth // 2), BF16),
            pltpu.SemaphoreType.DMA((3,)),
            pltpu.SemaphoreType.DMA((3,)),
            pltpu.SemaphoreType.DMA((5,)),
        ],
        compiler_params=pltpu.CompilerParams(vmem_limit_bytes=60 << 20),
        name="pack",
    )(block_image, dest_slot, core.reshape(1), tokens, out_weight.T)

    def shift(dx, dz):
        return [(x * 8 + z, (x + dx) % 4 * 8 + (z + dz) % 8) for x in range(4) for z in range(8)]

    z_groups = [[x * 8 + z for z in range(8)] for x in range(4)]
    z_line = lax.all_gather(qkv_weight, "grp", axis=0, tiled=True, axis_index_groups=z_groups)
    arrived = lax.all_to_all(outgoing, "grp", split_axis=0, concat_axis=0, tiled=True)
    offsets = (0, -1, -2, -3)
    x_line = jnp.concatenate(
        [out_half] + [lax.ppermute(out_half, "grp", shift(-dx, 0)) for dx in offsets[1:]], axis=0
    )
    out_rows = lax.all_gather(x_line, "grp", axis=0, tiled=True, axis_index_groups=z_groups)
    mods = modulation(timestep, mod_weight)
    hidden = pl.pallas_call(
        norm_kernel,
        out_shape=jax.ShapeDtypeStruct((rows, width + LANES), BF16),
        in_specs=[VMEM, VMEM],
        out_specs=VMEM,
        scratch_shapes=[pltpu.VMEM((rows, width), F32)],
        compiler_params=pltpu.CompilerParams(vmem_limit_bytes=24 << 20),
        cost_estimate=pl.CostEstimate(flops=66_000_000_000, bytes_accessed=2_000_000, transcendentals=0),
        name="norm",
    )(arrived, mods[:, : 2 * width])

    up = [(i, (i + 2) % members) for i in range(members)]
    down = [(i, (i - 2) % members) for i in range(members)]
    swap = [(i, i ^ 1) for i in range(members)]
    half_rows = rows // 2
    tie = lax.optimization_barrier
    x_below = lax.ppermute(z_line, "grp", shift(1, 0))
    x_above = lax.ppermute(z_line, "grp", shift(-1, 0))
    below = lax.ppermute(hidden, "uly", up)
    above = lax.ppermute(hidden, "uly", down)
    beside = lax.ppermute(hidden, "uly", swap)
    below, above, beside, x_below, x_above = tie((below, above, beside, x_below, x_above))
    far_a = lax.ppermute(below[:half_rows], "uly", up)
    far_b = lax.ppermute(above[half_rows:], "uly", down)
    below_s = lax.ppermute(below, "uly", swap)
    half_line = z_line.shape[0] // 2
    x_far_a = lax.ppermute(x_below[:half_line], "grp", shift(1, 0))
    x_far_b = lax.ppermute(x_above[half_line:], "grp", shift(-1, 0))
    far_a, far_b, below_s, above, x_far_a, x_far_b = tie((far_a, far_b, below_s, above, x_far_a, x_far_b))
    above_s = lax.ppermute(above, "uly", swap)
    far_as = lax.ppermute(far_a, "uly", swap)
    far_bs = lax.ppermute(far_b, "uly", swap)
    w_parts = [z_line, x_below, x_above, x_far_a, x_far_b]
    w_pieces = ((0, 0), (3, 0), (1, 0), (2, 0), (2, half_line))
    me = jnp.stack([g // 8, u // 2])
    parts = [hidden, beside, below, below_s, above, above_s, far_a, far_b, far_as, far_bs]
    pieces, at = [], 0
    for part in parts:
        pieces.append((at, part.shape[0]))
        at += part.shape[0]
    chip = 2 * rows
    mixed = pl.pallas_call(
        functools.partial(attention_kernel, tuple(pieces), w_pieces, chip),
        out_shape=[jax.ShapeDtypeStruct((chip, heads * HD), BF16)] * 4,
        in_specs=[SMEM, SMEM] + [HBM] * (len(parts) + len(w_parts)) + [VMEM, VMEM, HBM],
        out_specs=[VMEM] * 4,
        scratch_shapes=[
            pltpu.VMEM((group_tokens, width), BF16),
            pltpu.VMEM((group_tokens, LANES), BF16),
            pltpu.VMEM((width, 3 * heads * HD), BF16),
            pltpu.VMEM(text_kv.shape, BF16),
            pltpu.VMEM((group_tokens, 3 * heads * HD), F32),
            pltpu.VMEM((heads, group_tokens, HD), BF16),
            pltpu.VMEM((heads, group_tokens + IMG_GRP * TXT, HD), BF16),
            pltpu.VMEM((heads, group_tokens + IMG_GRP * TXT, HD), BF16),
            pltpu.SemaphoreType.DMA((4 * len(parts),)),
            pltpu.SemaphoreType.DMA((len(parts),)),
            pltpu.SemaphoreType.DMA((len(w_pieces),)),
            pltpu.SemaphoreType.DMA,
        ],
        compiler_params=pltpu.CompilerParams(vmem_limit_bytes=60 << 20),
        name="attention",
    )(me, txt_len, *parts, *w_parts, q_gain.reshape(1, HD), k_gain.reshape(1, HD), text_kv)

    from_up = lax.ppermute(mixed[1], "uly", down)
    from_down = lax.ppermute(mixed[2], "uly", up)
    from_far = lax.ppermute(mixed[3], "uly", [(i, (i + 4) % members) for i in range(members)])
    def product(low, kind, name):
        return pl.pallas_call(
            functools.partial(out_kernel, offsets, low),
            out_shape=jax.ShapeDtypeStruct((rows, width), kind),
            in_specs=[SMEM] + [VMEM] * 5,
            out_specs=VMEM,
            scratch_shapes=[pltpu.VMEM((rows, depth // 2), BF16)],
            compiler_params=pltpu.CompilerParams(vmem_limit_bytes=24 << 20),
            name=name,
        )(me, mixed[0], from_up, from_down, from_far, out_rows)

    send = product(rows, BF16, "out_send")
    keep = product(0, F32, "out_keep")
    came = lax.ppermute(send, "uly", swap)
    return pl.pallas_call(
        gate_kernel,
        grid=(2,),
        out_shape=jax.ShapeDtypeStruct((rows, width), BF16),
        in_specs=[
            pl.BlockSpec((rows, width // 2), lambda n: (0, n)),
            pl.BlockSpec((rows, width // 2), lambda n: (0, n)),
            pl.BlockSpec((rows, LANES), lambda n: (0, width // LANES)),
            pl.BlockSpec((IMG_GRP, width // 2), lambda n: (0, 4 + n)),
        ],
        out_specs=pl.BlockSpec((rows, width // 2), lambda n: (0, n)),
        compiler_params=pltpu.CompilerParams(vmem_limit_bytes=24 << 20),
        name="gate",
    )(keep, came, hidden, mods)


def solution(mesh):
    return jax.shard_map(
        body,
        mesh=mesh,
        in_specs=(
            P(("grp", "uly"), None),
            P(("grp", "uly")),
            P(("grp", "uly")),
            P("grp"),
            P("grp"),
            P(),
            P("grp", "uly"),
            P(),
            P(),
            P("grp", None, "uly"),
            P(None, "grp"),
        ),
        out_specs=P(("grp", "uly"), None),
        check_vma=False,
    )
```
